32 devices in a mesh: dp: 8 (over y, x, core), space: 4 (over z).
Axes of the slice: x: 2, y: 2, z: 4, core: 2. Of those that a mesh axis runs over, the one named last changes fastest.
Arguments:
- inputs: bfloat16 [8, 48, 128, 768], P('dp', 'space'), may hold values from -6 to 6
- gain: float32 [768], replicated, may hold values from 0.1 to 1.9
- w_in: bfloat16 [2, 768, 96], P(None, 'space'), may hold values from -0.4375 to 0.4375
- b_in: float32 [2, 768], P(None, 'space'), may hold values from -3 to 3
- w_out: bfloat16 [2, 768, 96], P(None, 'space'), may hold values from -0.4375 to 0.4375
- d_out: bfloat16 [8, 48, 128, 768], P('dp', 'space'), may hold values from -6 to 6
Outputs:
- d_inputs: bfloat16 [8, 48, 128, 768], P('dp', 'space')
- d_w_in: float32 [2, 768, 96], P(None, 'space')
- d_b_in: float32 [2, 768], P(None, 'space')
- d_w_out: float32 [2, 768, 96], P(None, 'space')
- d_gain: float32 [768], replicated
The draws below stay inside these ranges and needn't reach their ends.
All inputs are finite; a program needn't handle non-finite values.
Results may differ from the reference program's by a relative error of at most 0.012.
Values may be sent and summed in bfloat16 or wider, within the bound.
A program may use at most 128 MiB of HBM per device.

```python
import math
import jax
import jax.numpy as jnp
from jax import lax

H = 48
W = 128
C = 768
BLOCK = 96
SAMPLES = 8


def block_levels(own_key, dims, pieces, smallest, high):
    def one(dim, parts):
        heights = jax.random.uniform(jax.random.fold_in(jax.random.fold_in(own_key, 6), dim), (parts,), jnp.float32, smallest / len(pieces), high / len(pieces))
        return jnp.repeat(jnp.exp(heights), dims[dim] // parts).reshape((-1,) + (1,) * (len(dims) - dim - 1))

    level = one(*pieces[0])
    for cut in pieces[1:]:
        level = level * one(*cut)
    return level


def gaussian(key, dims, spread, bound, shards=(), kind=jnp.bfloat16):
    result = spread * jax.random.normal(key, dims, jnp.float32)
    if shards:
        result = result * block_levels(key, dims, shards, -0.22, 0.18)
    return jnp.clip(result, -bound, bound).astype(kind)


def setup_inputs(seed: int = 0) -> dict:
    arg_keys = jax.random.split(jax.random.key(seed), 7)
    return {
        "inputs": gaussian(arg_keys[0], (SAMPLES, H, W, C), 1.0, 6.0, ((0, 8), (1, 4))),
        "gain": jnp.clip(1.0 + 0.18 * jax.random.normal(arg_keys[1], (C,), jnp.float32), 0.1, 1.9),
        "w_in": gaussian(arg_keys[2], (2, C, BLOCK), (2 * BLOCK) ** -0.5, 0.4375, ((1, 4),)),
        "b_in": gaussian(arg_keys[3], (2, C), 0.5, 3.0, ((1, 4),), jnp.float32),
        "w_out": gaussian(arg_keys[4], (2, C, BLOCK), (2 * BLOCK) ** -0.5, 0.4375, ((1, 4),)),
        "d_out": gaussian(arg_keys[5], (SAMPLES, H, W, C), 1.0, 6.0, ((0, 8), (1, 4))),
    }


norm_eps = 1e-05
root_coef = math.sqrt(2.0 / math.pi)
cubic_coef = 0.044715

def dft_tables(length, kept):
    index_rows = jnp.arange(length, dtype=jnp.int32)
    index_cols = jnp.arange(kept, dtype=jnp.int32)
    product = index_rows[:, None] * index_cols[None, :] % length
    angles = 2.0 * math.pi / length * product.astype(jnp.float32)
    scale = 1.0 / math.sqrt(length)
    return (jnp.cos(angles) * scale, jnp.sin(angles) * scale)

def half_signs(kept):
    return jnp.concatenate([jnp.ones((kept,), jnp.float32), -jnp.ones((kept,), jnp.float32)])

def swap_parts(values, signs):
    return jnp.roll(values, values.shape[-1] // 2, axis=-1) * signs

def rows_apply(spectra, row_tables, signs):
    paired = jnp.einsum('tgh,shcm->tsgcm', row_tables.astype(jnp.float32), spectra.astype(jnp.float32), precision=lax.Precision.HIGHEST)
    return paired[0] + swap_parts(paired[1], signs)

def block_apply(values, weights, signs):
    operand = values.astype(jnp.float32)
    real_part = jnp.einsum('sgbim,bio->sgbom', operand, weights[0], precision=lax.Precision.HIGHEST)
    imag_part = jnp.einsum('sgbim,bio->sgbom', operand, weights[1], precision=lax.Precision.HIGHEST)
    return real_part + swap_parts(imag_part, signs)

def block_adjoint(values, weights, signs):
    operand = values.astype(jnp.float32)
    real_part = jnp.einsum('sgbom,bio->sgbim', operand, weights[0], precision=lax.Precision.HIGHEST)
    imag_part = jnp.einsum('sgbom,bio->sgbim', operand, weights[1], precision=lax.Precision.HIGHEST)
    return real_part + swap_parts(imag_part, signs)

def block_weight_grad(inputs_spec, grads_spec, signs):
    left = inputs_spec.astype(jnp.float32)
    right = grads_spec.astype(jnp.float32)
    real_part = jnp.einsum('sgbim,sgbom->bio', left, right, precision=lax.Precision.HIGHEST)
    imag_part = jnp.einsum('sgbim,sgbom->bio', swap_parts(left, signs), right, precision=lax.Precision.HIGHEST)
    return jnp.stack([real_part, imag_part])

def gelu_value(values):
    inner = root_coef * (values + cubic_coef * values * values * values)
    return 0.5 * values * (1.0 + jnp.tanh(inner))

def gelu_slope(values):
    inner = root_coef * (values + cubic_coef * values * values * values)
    tangent = jnp.tanh(inner)
    return 0.5 * (1.0 + tangent) + 0.5 * values * (1.0 - tangent * tangent) * root_coef * (1.0 + 3.0 * cubic_coef * values * values)

def reference(inputs, gain, w_in, b_in, w_out, d_out):
    samples, height, width, channels = inputs.shape
    kept = width // 2
    block = w_in.shape[2]
    groups = channels // block
    cos_rows, sin_rows = dft_tables(height, height)
    row_tables = jnp.stack([cos_rows, sin_rows]).astype(jnp.bfloat16)
    cos_cols, sin_cols = dft_tables(width, kept)
    forward_cols = jnp.concatenate([cos_cols, -sin_cols], axis=1).astype(jnp.bfloat16)
    doubling = jnp.where(jnp.arange(kept, dtype=jnp.int32) == 0, 1.0, 2.0).astype(jnp.float32)
    inverse_cols = jnp.concatenate([cos_cols * doubling, -sin_cols * doubling], axis=1).astype(jnp.bfloat16)
    forward_wide = forward_cols.astype(jnp.float32)
    inverse_wide = inverse_cols.astype(jnp.float32)
    plus_minus = half_signs(kept)
    minus_plus = -plus_minus
    weights_in = w_in.astype(jnp.float32).reshape(2, groups, block, block)
    weights_out = w_out.astype(jnp.float32).reshape(2, groups, block, block)
    bias_parts = b_in.reshape(2, groups, block)
    bias_full = jnp.concatenate([jnp.broadcast_to(bias_parts[0][:, :, None], (groups, block, kept)), jnp.broadcast_to(bias_parts[1][:, :, None], (groups, block, kept))], axis=-1)

    def per_sample(pair):
        sample_in, sample_grad = pair
        values = sample_in.astype(jnp.float32)[None]
        cotangent = sample_grad.astype(jnp.float32)[None]
        centre = lax.optimization_barrier(jnp.mean(values, axis=-1, keepdims=True))
        mean_removed = values - centre
        variance = lax.optimization_barrier(jnp.mean(mean_removed * mean_removed, axis=-1, keepdims=True))
        reciprocal_scale = lax.rsqrt(variance + norm_eps)
        standardized_input = mean_removed * reciprocal_scale
        normalized_input = (standardized_input * gain).astype(jnp.bfloat16)
        spectrum_cols = jnp.einsum('srwc,wm->srcm', normalized_input.astype(jnp.float32), forward_wide, precision=lax.Precision.HIGHEST).astype(jnp.bfloat16)
        modes = rows_apply(spectrum_cols, row_tables, plus_minus).astype(jnp.bfloat16)
        modes = modes.reshape(1, height, groups, block, width)
        preact = block_apply(modes, weights_in, minus_plus) + bias_full
        hidden = gelu_value(preact).astype(jnp.bfloat16)
        grad_cols = jnp.einsum('srwc,wm->srcm', cotangent, inverse_wide, precision=lax.Precision.HIGHEST).astype(jnp.bfloat16)
        grad_out = rows_apply(grad_cols, row_tables, plus_minus).astype(jnp.bfloat16)
        grad_out = grad_out.reshape(1, height, groups, block, width)
        grad_w_out = block_weight_grad(hidden, grad_out, minus_plus)
        d_hidden = block_adjoint(grad_out, weights_out, plus_minus)
        d_preact = (d_hidden * gelu_slope(preact)).astype(jnp.bfloat16)
        grad_w_in = block_weight_grad(modes, d_preact, minus_plus)
        bias_sums = lax.optimization_barrier(jnp.sum(d_preact.astype(jnp.float32).reshape(height, groups, block, 2, kept), axis=(0, 4)))
        grad_b_in = jnp.moveaxis(bias_sums, 2, 0).reshape(2, channels)
        d_modes = block_adjoint(d_preact, weights_in, plus_minus).astype(jnp.bfloat16)
        d_modes = d_modes.reshape(1, height, channels, width)
        d_spectrum = rows_apply(d_modes, row_tables, minus_plus).astype(jnp.bfloat16)
        d_filter = jnp.einsum('srcm,wm->srwc', d_spectrum.astype(jnp.float32), forward_wide, precision=lax.Precision.HIGHEST)
        normalized_gradient = cotangent + d_filter
        gain_gradient = lax.optimization_barrier(jnp.sum(normalized_gradient * standardized_input, axis=(0, 1, 2)))
        rescaled_output = normalized_gradient * gain
        value_gradient = reciprocal_scale * (rescaled_output - lax.optimization_barrier(jnp.mean(rescaled_output, axis=-1, keepdims=True)) - standardized_input * lax.optimization_barrier(jnp.mean(rescaled_output * standardized_input, axis=-1, keepdims=True)))
        return (value_gradient[0].astype(jnp.bfloat16), grad_w_in.reshape(2, channels, block), grad_b_in, grad_w_out.reshape(2, channels, block), gain_gradient)
    results = lax.map(per_sample, (inputs, d_out))
    return (results[0], lax.optimization_barrier(jnp.sum(results[1], axis=0)), lax.optimization_barrier(jnp.sum(results[2], axis=0)), lax.optimization_barrier(jnp.sum(results[3], axis=0)), lax.optimization_barrier(jnp.sum(results[4], axis=0)))
```

```python
import functools
import math

import jax
import jax.numpy as jnp
import ml_dtypes
import numpy as np
from jax import lax
from jax.experimental import pallas as pl
from jax.experimental.pallas import tpu as pltpu
from jax.sharding import PartitionSpec as P

norm_eps = 1e-05
root_coef = math.sqrt(2.0 / math.pi)
cubic_coef = 0.044715


def dft_tables(length, kept):
    index_rows = jnp.arange(length, dtype=jnp.int32)
    index_cols = jnp.arange(kept, dtype=jnp.int32)
    product = index_rows[:, None] * index_cols[None, :] % length
    angles = 2.0 * math.pi / length * product.astype(jnp.float32)
    scale = 1.0 / math.sqrt(length)
    return (jnp.cos(angles) * scale, jnp.sin(angles) * scale)


def half_signs(kept):
    return jnp.concatenate([jnp.ones((kept,), jnp.float32), -jnp.ones((kept,), jnp.float32)])


def swap_parts(values, signs):
    return jnp.roll(values, values.shape[-1] // 2, axis=-1) * signs.astype(values.dtype)


def rows_apply(spectra, row_tables, signs):
    paired = jnp.einsum("tgh,shcm->tsgcm", row_tables, spectra, preferred_element_type=jnp.float32)
    return paired[0] + swap_parts(paired[1], signs)


def block_apply(values, weights, signs):
    real_part = jnp.einsum(
        "sgbim,bio->sgbom", values, weights[0], preferred_element_type=jnp.float32
    )
    imag_part = jnp.einsum(
        "sgbim,bio->sgbom", values, weights[1], preferred_element_type=jnp.float32
    )
    return real_part + swap_parts(imag_part, signs)


def block_adjoint(values, weights, signs):
    real_part = jnp.einsum(
        "sgbom,bio->sgbim", values, weights[0], preferred_element_type=jnp.float32
    )
    imag_part = jnp.einsum(
        "sgbom,bio->sgbim", values, weights[1], preferred_element_type=jnp.float32
    )
    return real_part + swap_parts(imag_part, signs)


def block_weight_grad(inputs_spec, grads_spec, signs):
    real_part = jnp.einsum(
        "sgbim,sgbom->bio", inputs_spec, grads_spec, preferred_element_type=jnp.float32
    )
    imag_part = jnp.einsum(
        "sgbim,sgbom->bio",
        swap_parts(inputs_spec, signs),
        grads_spec,
        preferred_element_type=jnp.float32,
    )
    return jnp.stack([real_part, imag_part])


def gelu_value(values):
    inner = root_coef * (values + cubic_coef * values * values * values)
    return 0.5 * values * (1.0 + jnp.tanh(inner))


def gelu_slope(values):
    inner = root_coef * (values + cubic_coef * values * values * values)
    tangent = jnp.tanh(inner)
    return 0.5 * (1.0 + tangent) + 0.5 * values * (1.0 - tangent * tangent) * root_coef * (
        1.0 + 3.0 * cubic_coef * values * values
    )


def on_device(inputs, gain, w_in, b_in, w_out, d_out):
    samples, rows, width, channels = inputs.shape
    kept = width // 2
    height = rows * lax.axis_size("space")
    local_channels = w_in.shape[1]
    block = w_in.shape[2]
    groups = local_channels // block
    cos_rows, sin_rows = dft_tables(height, height)
    row_tables = jnp.stack([cos_rows, sin_rows]).astype(jnp.bfloat16)
    cos_cols, sin_cols = dft_tables(width, kept)
    forward_cols = jnp.concatenate([cos_cols, -sin_cols], axis=1).astype(jnp.bfloat16)
    doubling = jnp.where(jnp.arange(kept, dtype=jnp.int32) == 0, 1.0, 2.0).astype(jnp.float32)
    inverse_cols = jnp.concatenate([cos_cols * doubling, -sin_cols * doubling], axis=1).astype(
        jnp.bfloat16
    )
    plus_minus = half_signs(kept)
    minus_plus = -plus_minus
    weights_in = w_in.reshape(2, groups, block, block)
    weights_out = w_out.reshape(2, groups, block, block)
    bias_parts = b_in.reshape(2, groups, block)
    bias_full = jnp.concatenate(
        [
            jnp.broadcast_to(bias_parts[0][:, :, None], (groups, block, kept)),
            jnp.broadcast_to(bias_parts[1][:, :, None], (groups, block, kept)),
        ],
        axis=-1,
    )
    values = inputs.astype(jnp.float32)
    centre = jnp.mean(values, axis=-1, keepdims=True)
    mean_removed = values - centre
    variance = jnp.mean(mean_removed * mean_removed, axis=-1, keepdims=True)
    reciprocal_scale = lax.rsqrt(variance + norm_eps)
    standardized_input = mean_removed * reciprocal_scale
    normalized_input = (standardized_input * gain).astype(jnp.bfloat16)
    spectrum_cols = jnp.einsum(
        "srwc,wm->srcm", normalized_input, forward_cols, preferred_element_type=jnp.float32
    ).astype(jnp.bfloat16)
    spectrum_full = lax.all_to_all(spectrum_cols, "space", split_axis=2, concat_axis=1, tiled=True)
    modes = rows_apply(spectrum_full, row_tables, plus_minus).astype(jnp.bfloat16)
    modes = modes.reshape(samples, height, groups, block, width)
    preact = block_apply(modes, weights_in, minus_plus) + bias_full
    hidden = gelu_value(preact).astype(jnp.bfloat16)
    grad_cols = jnp.einsum(
        "srwc,wm->srcm", d_out, inverse_cols, preferred_element_type=jnp.float32
    ).astype(jnp.bfloat16)
    grad_full = lax.all_to_all(grad_cols, "space", split_axis=2, concat_axis=1, tiled=True)
    grad_out = rows_apply(grad_full, row_tables, plus_minus).astype(jnp.bfloat16)
    grad_out = grad_out.reshape(samples, height, groups, block, width)
    grad_w_out = block_weight_grad(hidden, grad_out, minus_plus)
    d_hidden = block_adjoint(grad_out, weights_out, plus_minus)
    d_preact = (d_hidden * gelu_slope(preact)).astype(jnp.bfloat16)
    grad_w_in = block_weight_grad(modes, d_preact, minus_plus)
    bias_sums = jnp.sum(
        d_preact.reshape(samples, height, groups, block, 2, kept), axis=(0, 1, 5), dtype=jnp.float32
    )
    grad_b_in = jnp.moveaxis(bias_sums, 2, 0).reshape(2, local_channels)
    d_modes = block_adjoint(d_preact, weights_in, plus_minus).astype(jnp.bfloat16)
    d_modes = d_modes.reshape(samples, height, local_channels, width)
    d_spectrum = rows_apply(d_modes, row_tables, minus_plus).astype(jnp.bfloat16)
    d_cols = lax.all_to_all(d_spectrum, "space", split_axis=1, concat_axis=2, tiled=True)
    d_filter = jnp.einsum("srcm,wm->srwc", d_cols, forward_cols, preferred_element_type=jnp.float32)
    normalized_gradient = d_out.astype(jnp.float32) + d_filter
    gain_component = jnp.sum(normalized_gradient * standardized_input, axis=(0, 1, 2))
    rescaled_output = normalized_gradient * gain
    value_gradient = reciprocal_scale * (
        rescaled_output
        - jnp.mean(rescaled_output, axis=-1, keepdims=True)
        - standardized_input
        * jnp.mean(rescaled_output * standardized_input, axis=-1, keepdims=True)
    )
    d_inputs = value_gradient.astype(jnp.bfloat16)
    flat_w_in = grad_w_in.reshape(2, local_channels, block)
    flat_w_out = grad_w_out.reshape(2, local_channels, block)
    sum_w_in, sum_b_in, sum_w_out = lax.psum((flat_w_in, grad_b_in, flat_w_out), "dp")
    sum_gain = lax.psum(gain_component, ("dp", "space"))
    return (d_inputs, sum_w_in, sum_b_in, sum_w_out, sum_gain)


MESH = pl.DeviceIdType.MESH
BF = jnp.bfloat16
F32 = jnp.float32
NT = (((1,), (1,)), ((), ()))
TN = (((0,), (0,)), ((), ()))
K8 = 8


def np_tables(length, kept):
    product = (np.arange(length)[:, None] * np.arange(kept)[None, :]) % length
    angles = (2.0 * np.pi / length) * product
    scale = 1.0 / np.sqrt(length)
    return np.cos(angles) * scale, np.sin(angles) * scale


def narrow(table):
    return table.astype(np.float32).astype(ml_dtypes.bfloat16)


def column_tables(width, kept):
    cos, sin = np_tables(width, kept)
    order = np.arange(width)
    wave = (order // (4 * K8)) * (2 * K8) + (order // (2 * K8)) % 2 * K8 + order % K8
    part = (order // K8) % 2
    forward = np.where(part[:, None] == 0, cos.T[wave], -sin.T[wave])
    double = np.where(wave == 0, 1.0, 2.0)[:, None]
    return narrow(forward), narrow(forward * double), narrow(forward.T)


def row_matrix(height):
    cos, sin = np_tables(height, height)
    row = np.arange(2 * height * K8)
    rp, rg, rk = row // (height * K8), row % (height * K8) // K8, row % K8
    cp, ch, ck = row // K8 % 2, row // (2 * K8), row % K8
    c = cos[rg[:, None], ch[None, :]]
    s = sin[rg[:, None], ch[None, :]]
    signed = np.where(rp[:, None] < cp[None, :], s, -s)
    full = np.where(rp[:, None] == cp[None, :], c, signed)
    full = np.where(rk[:, None] == ck[None, :], full, 0.0)
    return narrow(full), narrow(full.T)


def lane_maps(local, block):
    picks, folds, masks = [], [], []
    lane = np.arange(2 * local)
    wide = lane < 256
    half = np.where(wide, lane // 128, (lane - 256) // 64)
    even = np.where(wide, lane % 128, 128 + lane % 64)
    odd = np.where(wide, 64 + lane % 128, lane % 64)
    for channel in (even, odd):
        picks.append(channel[:, None] == np.arange(local)[None, :])
        folds.append(channel[:, None] % block == np.arange(128)[None, :])
        group = channel // block
        masks.append(
            (half[:, None] == half[None, :]) & (group[:, None] == group[None, :])
        )
    return tuple(narrow(np.stack(v)) for v in (picks, folds, masks))


def kernel(
    ndp,
    nsp,
    x_ref,
    dout_ref,
    gain_ref,
    win_ref,
    bin_ref,
    wout_ref,
    fwd_ref,
    inv_ref,
    fin_ref,
    m1_ref,
    m2_ref,
    e_ref,
    e2_ref,
    mask_ref,
    dx_ref,
    gw_ref,
    gg_ref,
    send,
    recv,
    dsend,
    drecv,
    wci,
    wco,
    bias,
    modes,
    gout,
    hidden,
    dpre,
    dmodes,
    acc_in,
    acc_out,
    acc_b,
    mean_s,
    rstd_s,
    dd,
    part_g,
    recv_g,
    gain_a,
    gain_b,
    gain_c,
    in_send,
    in_recv,
    d_send,
    d_recv,
    rs_send,
    rs_recv,
    ag_send,
    ag_recv,
    ga_send,
    ga_recv,
    gb_send,
    gb_recv,
):
    dp = lax.axis_index("dp")
    me = lax.axis_index("space")
    rows = x_ref.shape[0]
    chunks = send.shape[1]
    pos = modes.shape[0]
    lanes = wci.shape[0] // 2
    sps = [lax.rem(me + o, nsp) for o in range(1, nsp)]
    dps = [lax.rem(dp + o, ndp) for o in range(1, ndp)]
    parity = lax.rem(me, 2)

    barrier = pltpu.get_barrier_semaphore()
    for z in sps:
        pl.semaphore_signal(barrier, inc=1, device_id={"space": z}, device_id_type=MESH)
    for q in dps:
        pl.semaphore_signal(barrier, inc=1, device_id={"dp": q}, device_id_type=MESH)
    pl.semaphore_wait(barrier, nsp + ndp - 2)

    def in_copy(a, j, z, slot):
        return pltpu.make_async_remote_copy(
            src_ref=send.at[a, j, z],
            dst_ref=recv.at[a, j, slot],
            send_sem=in_send.at[a, j, z],
            recv_sem=in_recv.at[a, j, slot],
            device_id={"space": z},
            device_id_type=MESH,
        )

    def d_copy(j, z, slot):
        return pltpu.make_async_remote_copy(
            src_ref=dsend.at[j, z],
            dst_ref=drecv.at[j, slot],
            send_sem=d_send.at[j, z],
            recv_sem=d_recv.at[j, slot],
            device_id={"space": z},
            device_id_type=MESH,
        )

    low = lax.broadcasted_iota(jnp.int32, (chunks * 16, 128), 1) < 64

    def pack(y, a, r):
        y = y.reshape(chunks, 2, 16, y.shape[-1])
        for q in range(nsp // 2):
            b = 384 * q

            def tile(t, half):
                return y[:, half, :, b + 128 * t : b + 128 * t + 128].reshape(chunks * 16, 128)

            def put(d, t, v):
                v = v.astype(BF).reshape(chunks, 16, 128)
                send[a, :, 2 * q + d, r, :, 128 * t : 128 * t + 128] = v

            b0, b1 = tile(1, 0), tile(1, 1)
            put(0, 0, tile(0, 0))
            put(0, 1, tile(0, 1))
            put(0, 2, jnp.where(low, b0, pltpu.roll(b1, 64, 1)))
            put(1, 0, tile(2, 0))
            put(1, 1, tile(2, 1))
            put(1, 2, jnp.where(low, pltpu.roll(b0, 64, 1), b1))

    def start_in(a, j):
        for z in sps:
            in_copy(a, j, z, me).start()
        recv[a, j, me] = send[a, j, me]

    def grad_row(r, c):
        pack(jnp.dot(inv_ref[...], dout_ref[r], preferred_element_type=F32), 1, r)
        return c

    lax.fori_loop(0, rows, grad_row, 0)
    start_in(1, 0)

    gain = gain_ref[...]

    def norm_row(r, c):
        v = x_ref[r].astype(F32)
        mean = jnp.mean(v, axis=-1, keepdims=True)
        v = v - mean
        rstd = lax.rsqrt(jnp.mean(v * v, axis=-1, keepdims=True) + norm_eps)
        mean_s[r] = mean
        rstd_s[r] = rstd
        normed = (v * rstd * gain).astype(BF)
        pack(jnp.dot(fwd_ref[...], normed, preferred_element_type=F32), 0, r)
        return c

    lax.fori_loop(0, rows, norm_row, 0)
    start_in(0, 0)

    pick = e_ref[parity]
    fold = e2_ref[parity]
    mask = mask_ref[parity]
    for w_ref, out in ((win_ref, wci), (wout_ref, wco)):
        block = w_ref.shape[2]
        for p in range(2):
            w = jnp.dot(pick, w_ref[p], preferred_element_type=F32).astype(BF)
            w = lax.dot_general(w, fold[:, :block], NT, preferred_element_type=F32).astype(BF)
            w = w * mask
            if p == 0:
                out[:lanes, :lanes] = w
                out[lanes:, lanes:] = w
            else:
                out[:lanes, lanes:] = w
                out[lanes:, :lanes] = -w
    wide = lax.dot_general(
        bin_ref[...], pick.astype(F32), NT, precision=lax.Precision.HIGHEST,
        preferred_element_type=F32,
    )
    bias[:, :lanes] = wide[0:1]
    bias[:, lanes:] = wide[1:2]
    acc_in[...] = jnp.zeros_like(acc_in)
    acc_out[...] = jnp.zeros_like(acc_out)
    acc_b[...] = jnp.zeros_like(acc_b)

    tile_rows = 128

    def middle(j):
        for a, out in ((1, gout), (0, modes)):
            for z in sps:
                in_copy(a, j, z, z).wait_recv()
            x = recv[a, j].reshape(2 * pos, lanes)
            for p in range(2):
                t = jnp.dot(m1_ref[p * pos : (p + 1) * pos], x, preferred_element_type=F32)
                out[:, p * lanes : (p + 1) * lanes] = t.astype(BF)

        def tile(t, c):
            at = pl.ds(pl.multiple_of(t * tile_rows, tile_rows), tile_rows)
            v = jnp.dot(modes[at], wci[...], preferred_element_type=F32) + bias[...]
            dh = lax.dot_general(gout[at], wco[...], NT, preferred_element_type=F32)
            tangent = jnp.tanh(root_coef * (v + cubic_coef * v * v * v))
            hidden[at] = (0.5 * v * (1.0 + tangent)).astype(BF)
            slope = 0.5 * (1.0 + tangent) + 0.5 * v * (1.0 - tangent * tangent) * root_coef * (
                1.0 + 3.0 * cubic_coef * v * v
            )
            d = (dh * slope).astype(BF)
            dpre[at] = d
            wide = d.astype(F32).reshape(tile_rows // 8, 8, 2 * lanes)
            acc_b[...] += jnp.sum(wide, axis=0)
            dm = lax.dot_general(d, wci[...], NT, preferred_element_type=F32).astype(BF)
            dmodes[at] = dm[:, :lanes]
            low_at = pl.ds(pl.multiple_of(pos + t * tile_rows, tile_rows), tile_rows)
            dmodes[low_at] = dm[:, lanes:]
            return c

        lax.fori_loop(0, pos // tile_rows, tile, 0)
        ds = jnp.dot(m2_ref[...], dmodes[...], preferred_element_type=F32).astype(BF)
        dsend[j] = ds.reshape(nsp, rows, 16, lanes)
        for z in sps:
            d_copy(j, z, me).start()
        drecv[j, me] = dsend[j, me]
        acc_out[...] += lax.dot_general(hidden[...], gout[...], TN, preferred_element_type=F32)
        acc_in[...] += lax.dot_general(modes[...], dpre[...], TN, preferred_element_type=F32)

    def step(j, c):
        @pl.when(j + 1 < chunks)
        def _():
            start_in(1, j + 1)
            start_in(0, j + 1)

        middle(j)
        return c

    lax.fori_loop(0, chunks, step, 0)

    local = e_ref.shape[2]
    shard = part_g.shape[1]
    pick32 = pick.astype(F32)
    fold32 = fold.astype(F32)
    mask32 = mask.astype(F32)
    sums_b = jnp.sum(acc_b[...], axis=0, keepdims=True)
    column = lax.broadcasted_iota(jnp.int32, (local, 128), 1)
    flat = []
    for n, acc in enumerate((acc_in, acc_out)):
        full = (
            acc[:lanes, :lanes] + acc[lanes:, lanes:],
            acc[:lanes, lanes:] - acc[lanes:, :lanes],
        )
        for p in range(2):
            g = lax.dot_general(
                pick32, full[p] * mask32, TN, precision=lax.Precision.HIGHEST,
                preferred_element_type=F32,
            )
            g = jnp.dot(g, fold32, precision=lax.Precision.HIGHEST, preferred_element_type=F32)
            if n == 0:
                db = lax.dot_general(
                    pick32, jnp.broadcast_to(sums_b[:, p * lanes : (p + 1) * lanes], (128, lanes)),
                    (((0,), (1,)), ((), ())), precision=lax.Precision.HIGHEST,
                    preferred_element_type=F32,
                )
                g = jnp.where(column == 96, db, g)
            per = local // shard
            part_g[(2 * n + p) * per : (2 * n + p + 1) * per] = g.reshape(per, shard, 128)

    def rs_copy(q, slot):
        return pltpu.make_async_remote_copy(
            src_ref=part_g.at[q],
            dst_ref=recv_g.at[slot],
            send_sem=rs_send.at[q],
            recv_sem=rs_recv.at[slot],
            device_id={"dp": q},
            device_id_type=MESH,
        )

    def ag_copy(q, slot):
        return pltpu.make_async_remote_copy(
            src_ref=gw_ref.at[dp],
            dst_ref=gw_ref.at[slot],
            send_sem=ag_send.at[q],
            recv_sem=ag_recv.at[slot],
            device_id={"dp": q},
            device_id_type=MESH,
        )

    for q in dps:
        rs_copy(q, dp).start()
    recv_g[dp] = part_g[dp]
    for q in dps:
        rs_copy(q, q).wait_recv()
    gw_ref[dp] = jnp.sum(recv_g[...], axis=0)
    for q in dps:
        ag_copy(q, dp).start()

    for j in range(chunks):
        for z in sps:
            d_copy(j, z, z).wait_recv()

    def last_row(r, c):
        for q in range(nsp // 2):
            b = 384 * q

            def tile(d, t):
                v = drecv[:, 2 * q + d, r, :, 128 * t : 128 * t + 128]
                return v.reshape(chunks * 16, 128)

            def put(half, t, v):
                v = v.astype(BF).reshape(chunks, 16, 128)
                dd[:, half, :, b + 128 * t : b + 128 * t + 128] = v

            e2, o2 = tile(0, 2).astype(F32), tile(1, 2).astype(F32)
            for half in range(2):
                put(half, 0, tile(0, half))
                put(half, 2, tile(1, half))
            put(0, 1, jnp.where(low, e2, pltpu.roll(o2, 64, 1)))
            put(1, 1, jnp.where(low, pltpu.roll(e2, 64, 1), o2))
        spectrum = dd[...].reshape(chunks * 32, dd.shape[-1])
        grad = jnp.dot(fin_ref[...], spectrum, preferred_element_type=F32)
        grad = grad + dout_ref[r].astype(F32)
        rstd = rstd_s[r]
        xhat = (x_ref[r].astype(F32) - mean_s[r]) * rstd
        prod = grad * xhat
        c = c + jnp.sum(prod.reshape(-1, 8, prod.shape[-1]), axis=0)
        scaled = grad * gain
        m_a = jnp.mean(scaled, axis=-1, keepdims=True)
        m_b = jnp.mean(prod * gain, axis=-1, keepdims=True)
        dx_ref[r] = (rstd * (scaled - m_a - xhat * m_b)).astype(BF)
        return c

    gain_sum = lax.fori_loop(0, rows, last_row, jnp.zeros((8, x_ref.shape[-1]), F32))

    def ga_copy(z, slot):
        return pltpu.make_async_remote_copy(
            src_ref=gain_a.at[me],
            dst_ref=gain_a.at[slot],
            send_sem=ga_send.at[z],
            recv_sem=ga_recv.at[slot],
            device_id={"space": z},
            device_id_type=MESH,
        )

    def gb_copy(q, slot):
        return pltpu.make_async_remote_copy(
            src_ref=gain_b.at[dp],
            dst_ref=gain_b.at[slot],
            send_sem=gb_send.at[q],
            recv_sem=gb_recv.at[slot],
            device_id={"dp": q},
            device_id_type=MESH,
        )

    gain_a[me] = gain_sum
    for z in sps:
        ga_copy(z, me).start()
    for z in sps:
        ga_copy(z, z).wait_recv()
    gain_b[dp] = jnp.sum(gain_a[...], axis=0)
    for q in dps:
        gb_copy(q, dp).start()
    for q in dps:
        gb_copy(q, q).wait_recv()
    gg_ref[...] = jnp.sum(jnp.sum(gain_b[...], axis=0), axis=0, keepdims=True)

    for q in dps:
        ag_copy(q, q).wait_recv()
    for q in dps:
        rs_copy(q, dp).wait_send()
        ag_copy(q, dp).wait_send()
        gb_copy(q, dp).wait_send()
    for z in sps:
        ga_copy(z, me).wait_send()

    def drain(j, c):
        for z in sps:
            in_copy(0, j, z, me).wait_send()
            in_copy(1, j, z, me).wait_send()
            d_copy(j, z, me).wait_send()
        return c

    lax.fori_loop(0, chunks, drain, 0)


def fused(ndp, nsp, inputs, gain, w_in, b_in, w_out, d_out):
    _, rows, width, channels = inputs.shape
    kept = width // 2
    height = rows * nsp
    local, block = w_in.shape[1], w_in.shape[2]
    chunks = kept // (2 * K8)
    lanes = 2 * local
    pos = height * K8
    shard = 4 * local // ndp
    fwd, inv, fin = column_tables(width, kept)
    m1, m2 = row_matrix(height)
    pick, fold, mask = lane_maps(local, block)
    vmem = pl.BlockSpec(memory_space=pltpu.VMEM)
    dma = pltpu.SemaphoreType.DMA
    dx, gw, gg = pl.pallas_call(
        functools.partial(kernel, ndp, nsp),
        out_shape=(
            jax.ShapeDtypeStruct((rows, width, channels), BF),
            jax.ShapeDtypeStruct((ndp, shard, 128), F32),
            jax.ShapeDtypeStruct((1, channels), F32),
        ),
        in_specs=[vmem] * 14,
        out_specs=(vmem, vmem, vmem),
        scratch_shapes=[
            pltpu.VMEM((2, chunks, nsp, rows, 16, lanes), BF),
            pltpu.VMEM((2, chunks, nsp, rows, 16, lanes), BF),
            pltpu.VMEM((chunks, nsp, rows, 16, lanes), BF),
            pltpu.VMEM((chunks, nsp, rows, 16, lanes), BF),
            pltpu.VMEM((2 * lanes, 2 * lanes), BF),
            pltpu.VMEM((2 * lanes, 2 * lanes), BF),
            pltpu.VMEM((1, 2 * lanes), F32),
            pltpu.VMEM((pos, 2 * lanes), BF),
            pltpu.VMEM((pos, 2 * lanes), BF),
            pltpu.VMEM((pos, 2 * lanes), BF),
            pltpu.VMEM((pos, 2 * lanes), BF),
            pltpu.VMEM((2 * pos, lanes), BF),
            pltpu.VMEM((2 * lanes, 2 * lanes), F32),
            pltpu.VMEM((2 * lanes, 2 * lanes), F32),
            pltpu.VMEM((8, 2 * lanes), F32),
            pltpu.VMEM((rows, width, 1), F32),
            pltpu.VMEM((rows, width, 1), F32),
            pltpu.VMEM((chunks, 2, 16, channels), BF),
            pltpu.VMEM((ndp, shard, 128), F32),
            pltpu.VMEM((ndp, shard, 128), F32),
            pltpu.VMEM((nsp, 8, channels), F32),
            pltpu.VMEM((ndp, 8, channels), F32),
            pltpu.VMEM((8, channels), F32),
            dma((2, chunks, nsp)),
            dma((2, chunks, nsp)),
            dma((chunks, nsp)),
            dma((chunks, nsp)),
            dma((ndp,)),
            dma((ndp,)),
            dma((ndp,)),
            dma((ndp,)),
            dma((nsp,)),
            dma((nsp,)),
            dma((ndp,)),
            dma((ndp,)),
        ],
        compiler_params=pltpu.CompilerParams(
            collective_id=0, has_side_effects=True, vmem_limit_bytes=60 * 1024 * 1024
        ),
    )(
        inputs[0],
        d_out[0],
        gain[None, :],
        w_in,
        b_in,
        w_out,
        *(jnp.asarray(v) for v in (fwd, inv, fin, m1, m2, pick, fold, mask)),
    )
    gw = gw.reshape(4, local, 128)
    return (
        dx[None],
        gw[:2, :, :block],
        gw[:2, :, block],
        gw[2:, :, :block],
        gg[0],
    )


def choose(ndp, nsp, *args):
    inputs, w_in = args[0], args[2]
    local, block = w_in.shape[1], w_in.shape[2]
    fits = (
        inputs.shape[0] == 1
        and nsp == 4
        and local == 192
        and block == 96
        and inputs.shape[2] % 32 == 0
        and inputs.shape[1] * nsp * K8 % 128 == 0
        and local % (4 * local // ndp) == 0
        and (4 * local // ndp) % 8 == 0
    )
    if fits:
        return fused(ndp, nsp, *args)
    return on_device(*args)


def solution(mesh):
    return jax.shard_map(
        functools.partial(choose, mesh.shape["dp"], mesh.shape["space"]),
        mesh=mesh,
        in_specs=(
            P("dp", "space", None, None),
            P(),
            P(None, "space", None),
            P(None, "space"),
            P(None, "space", None),
            P("dp", "space", None, None),
        ),
        out_specs=(
            P("dp", "space", None, None),
            P(None, "space", None),
            P(None, "space"),
            P(None, "space", None),
            P(),
        ),
        check_vma=False,
    )
```

```python
import functools
import math

import jax
import jax.numpy as jnp
import ml_dtypes
import numpy as np
from jax import lax
from jax.experimental import pallas as pl
from jax.experimental.pallas import tpu as pltpu
from jax.sharding import PartitionSpec as P

norm_eps = 1e-05
root_coef = math.sqrt(2.0 / math.pi)
cubic_coef = 0.044715


def dft_tables(length, kept):
    index_rows = jnp.arange(length, dtype=jnp.int32)
    index_cols = jnp.arange(kept, dtype=jnp.int32)
    product = index_rows[:, None] * index_cols[None, :] % length
    angles = 2.0 * math.pi / length * product.astype(jnp.float32)
    scale = 1.0 / math.sqrt(length)
    return (jnp.cos(angles) * scale, jnp.sin(angles) * scale)


def half_signs(kept):
    return jnp.concatenate([jnp.ones((kept,), jnp.float32), -jnp.ones((kept,), jnp.float32)])


def swap_parts(values, signs):
    return jnp.roll(values, values.shape[-1] // 2, axis=-1) * signs.astype(values.dtype)


def rows_apply(spectra, row_tables, signs):
    paired = jnp.einsum("tgh,shcm->tsgcm", row_tables, spectra, preferred_element_type=jnp.float32)
    return paired[0] + swap_parts(paired[1], signs)


def block_apply(values, weights, signs):
    real_part = jnp.einsum(
        "sgbim,bio->sgbom", values, weights[0], preferred_element_type=jnp.float32
    )
    imag_part = jnp.einsum(
        "sgbim,bio->sgbom", values, weights[1], preferred_element_type=jnp.float32
    )
    return real_part + swap_parts(imag_part, signs)


def block_adjoint(values, weights, signs):
    real_part = jnp.einsum(
        "sgbom,bio->sgbim", values, weights[0], preferred_element_type=jnp.float32
    )
    imag_part = jnp.einsum(
        "sgbom,bio->sgbim", values, weights[1], preferred_element_type=jnp.float32
    )
    return real_part + swap_parts(imag_part, signs)


def block_weight_grad(inputs_spec, grads_spec, signs):
    real_part = jnp.einsum(
        "sgbim,sgbom->bio", inputs_spec, grads_spec, preferred_element_type=jnp.float32
    )
    imag_part = jnp.einsum(
        "sgbim,sgbom->bio",
        swap_parts(inputs_spec, signs),
        grads_spec,
        preferred_element_type=jnp.float32,
    )
    return jnp.stack([real_part, imag_part])


def gelu_value(values):
    inner = root_coef * (values + cubic_coef * values * values * values)
    return 0.5 * values * (1.0 + jnp.tanh(inner))


def gelu_slope(values):
    inner = root_coef * (values + cubic_coef * values * values * values)
    tangent = jnp.tanh(inner)
    return 0.5 * (1.0 + tangent) + 0.5 * values * (1.0 - tangent * tangent) * root_coef * (
        1.0 + 3.0 * cubic_coef * values * values
    )


def on_device(inputs, gain, w_in, b_in, w_out, d_out):
    samples, rows, width, channels = inputs.shape
    kept = width // 2
    height = rows * lax.axis_size("space")
    local_channels = w_in.shape[1]
    block = w_in.shape[2]
    groups = local_channels // block
    cos_rows, sin_rows = dft_tables(height, height)
    row_tables = jnp.stack([cos_rows, sin_rows]).astype(jnp.bfloat16)
    cos_cols, sin_cols = dft_tables(width, kept)
    forward_cols = jnp.concatenate([cos_cols, -sin_cols], axis=1).astype(jnp.bfloat16)
    doubling = jnp.where(jnp.arange(kept, dtype=jnp.int32) == 0, 1.0, 2.0).astype(jnp.float32)
    inverse_cols = jnp.concatenate([cos_cols * doubling, -sin_cols * doubling], axis=1).astype(
        jnp.bfloat16
    )
    plus_minus = half_signs(kept)
    minus_plus = -plus_minus
    weights_in = w_in.reshape(2, groups, block, block)
    weights_out = w_out.reshape(2, groups, block, block)
    bias_parts = b_in.reshape(2, groups, block)
    bias_full = jnp.concatenate(
        [
            jnp.broadcast_to(bias_parts[0][:, :, None], (groups, block, kept)),
            jnp.broadcast_to(bias_parts[1][:, :, None], (groups, block, kept)),
        ],
        axis=-1,
    )
    values = inputs.astype(jnp.float32)
    centre = jnp.mean(values, axis=-1, keepdims=True)
    mean_removed = values - centre
    variance = jnp.mean(mean_removed * mean_removed, axis=-1, keepdims=True)
    reciprocal_scale = lax.rsqrt(variance + norm_eps)
    standardized_input = mean_removed * reciprocal_scale
    normalized_input = (standardized_input * gain).astype(jnp.bfloat16)
    spectrum_cols = jnp.einsum(
        "srwc,wm->srcm", normalized_input, forward_cols, preferred_element_type=jnp.float32
    ).astype(jnp.bfloat16)
    spectrum_full = lax.all_to_all(spectrum_cols, "space", split_axis=2, concat_axis=1, tiled=True)
    modes = rows_apply(spectrum_full, row_tables, plus_minus).astype(jnp.bfloat16)
    modes = modes.reshape(samples, height, groups, block, width)
    preact = block_apply(modes, weights_in, minus_plus) + bias_full
    hidden = gelu_value(preact).astype(jnp.bfloat16)
    grad_cols = jnp.einsum(
        "srwc,wm->srcm", d_out, inverse_cols, preferred_element_type=jnp.float32
    ).astype(jnp.bfloat16)
    grad_full = lax.all_to_all(grad_cols, "space", split_axis=2, concat_axis=1, tiled=True)
    grad_out = rows_apply(grad_full, row_tables, plus_minus).astype(jnp.bfloat16)
    grad_out = grad_out.reshape(samples, height, groups, block, width)
    grad_w_out = block_weight_grad(hidden, grad_out, minus_plus)
    d_hidden = block_adjoint(grad_out, weights_out, plus_minus)
    d_preact = (d_hidden * gelu_slope(preact)).astype(jnp.bfloat16)
    grad_w_in = block_weight_grad(modes, d_preact, minus_plus)
    bias_sums = jnp.sum(
        d_preact.reshape(samples, height, groups, block, 2, kept), axis=(0, 1, 5), dtype=jnp.float32
    )
    grad_b_in = jnp.moveaxis(bias_sums, 2, 0).reshape(2, local_channels)
    d_modes = block_adjoint(d_preact, weights_in, plus_minus).astype(jnp.bfloat16)
    d_modes = d_modes.reshape(samples, height, local_channels, width)
    d_spectrum = rows_apply(d_modes, row_tables, minus_plus).astype(jnp.bfloat16)
    d_cols = lax.all_to_all(d_spectrum, "space", split_axis=1, concat_axis=2, tiled=True)
    d_filter = jnp.einsum("srcm,wm->srwc", d_cols, forward_cols, preferred_element_type=jnp.float32)
    normalized_gradient = d_out.astype(jnp.float32) + d_filter
    gain_component = jnp.sum(normalized_gradient * standardized_input, axis=(0, 1, 2))
    rescaled_output = normalized_gradient * gain
    value_gradient = reciprocal_scale * (
        rescaled_output
        - jnp.mean(rescaled_output, axis=-1, keepdims=True)
        - standardized_input
        * jnp.mean(rescaled_output * standardized_input, axis=-1, keepdims=True)
    )
    d_inputs = value_gradient.astype(jnp.bfloat16)
    flat_w_in = grad_w_in.reshape(2, local_channels, block)
    flat_w_out = grad_w_out.reshape(2, local_channels, block)
    sum_w_in, sum_b_in, sum_w_out = lax.psum((flat_w_in, grad_b_in, flat_w_out), "dp")
    sum_gain = lax.psum(gain_component, ("dp", "space"))
    return (d_inputs, sum_w_in, sum_b_in, sum_w_out, sum_gain)


MESH = pl.DeviceIdType.MESH
BF = jnp.bfloat16
F32 = jnp.float32
NT = (((1,), (1,)), ((), ()))
TN = (((0,), (0,)), ((), ()))
K8 = 8


def np_tables(length, kept):
    product = (np.arange(length)[:, None] * np.arange(kept)[None, :]) % length
    angles = (2.0 * np.pi / length) * product
    scale = 1.0 / np.sqrt(length)
    return np.cos(angles) * scale, np.sin(angles) * scale


def narrow(table):
    return table.astype(np.float32).astype(ml_dtypes.bfloat16)


def column_tables(width, kept):
    cos, sin = np_tables(width, kept)
    order = np.arange(width)
    wave = (order // (4 * K8)) * (2 * K8) + (order // (2 * K8)) % 2 * K8 + order % K8
    part = (order // K8) % 2
    forward = np.where(part[:, None] == 0, cos.T[wave], -sin.T[wave])
    double = np.where(wave == 0, 1.0, 2.0)[:, None]
    return narrow(forward), narrow(forward * double), narrow(forward.T)


def row_matrix(height):
    cos, sin = np_tables(height, height)
    row = np.arange(2 * height * K8)
    rp, rg, rk = row // (height * K8), row % (height * K8) // K8, row % K8
    cp, ch, ck = row // K8 % 2, row // (2 * K8), row % K8
    c = cos[rg[:, None], ch[None, :]]
    s = sin[rg[:, None], ch[None, :]]
    signed = np.where(rp[:, None] < cp[None, :], s, -s)
    full = np.where(rp[:, None] == cp[None, :], c, signed)
    full = np.where(rk[:, None] == ck[None, :], full, 0.0)
    return narrow(full), narrow(full.T)


def lane_maps(local, block):
    picks, folds, masks = [], [], []
    lane = np.arange(2 * local)
    wide = lane < 256
    half = np.where(wide, lane // 128, (lane - 256) // 64)
    even = np.where(wide, lane % 128, 128 + lane % 64)
    odd = np.where(wide, 64 + lane % 128, lane % 64)
    for channel in (even, odd):
        picks.append(channel[:, None] == np.arange(local)[None, :])
        folds.append(channel[:, None] % block == np.arange(128)[None, :])
        group = channel // block
        masks.append(
            (half[:, None] == half[None, :]) & (group[:, None] == group[None, :])
        )
    return tuple(narrow(np.stack(v)) for v in (picks, folds, masks))


def kernel(
    ndp,
    nsp,
    x_hbm,
    dout_hbm,
    gain_ref,
    win_ref,
    bin_ref,
    wout_ref,
    fwd_ref,
    inv_ref,
    fin_ref,
    m1_hbm,
    m2_hbm,
    e_hbm,
    e2_hbm,
    mask_hbm,
    dx_hbm,
    gw_ref,
    gg_ref,
    send,
    recv,
    dsend,
    drecv,
    wci,
    wco,
    bias,
    modes,
    gout,
    hidden,
    dpre,
    dmodes,
    acc_in,
    acc_out,
    acc_b,
    mean_s,
    rstd_s,
    dd,
    part_g,
    recv_g,
    gain_a,
    gain_b,
    acc_g,
    x_ref,
    dout_ref,
    m1_ref,
    m2_ref,
    e_ref,
    e2_ref,
    mask_ref,
    dx_ref,
    load_sem,
    store_sem,
    in_send,
    in_recv,
    d_send,
    d_recv,
    rs_send,
    rs_recv,
    ag_send,
    ag_recv,
    ga_send,
    ga_recv,
    gb_send,
    gb_recv,
):
    dp = lax.axis_index("dp")
    me = lax.axis_index("space")
    rows = x_ref.shape[0]
    chunks = send.shape[1]
    pos = modes.shape[0]
    lanes = wci.shape[0] // 2
    sps = [lax.rem(me + o, nsp) for o in range(1, nsp)]
    dps = [lax.rem(dp + o, ndp) for o in range(1, ndp)]
    parity = lax.rem(me, 2)
    part = rows // 2

    def load(n, src, dst):
        return pltpu.make_async_copy(src, dst, load_sem.at[n])

    def halves(ref, hf):
        return ref.at[pl.ds(hf * part, part)]

    loads = [load(hf, halves(dout_hbm, hf), halves(dout_ref, hf)) for hf in range(2)]
    loads += [load(2 + hf, halves(x_hbm, hf), halves(x_ref, hf)) for hf in range(2)]
    pairs = ((e_hbm, e_ref), (e2_hbm, e2_ref), (mask_hbm, mask_ref), (m1_hbm, m1_ref), (m2_hbm, m2_ref))
    loads += [load(4 + n, src, dst) for n, (src, dst) in enumerate(pairs)]
    for copy in loads:
        copy.start()

    barrier = pltpu.get_barrier_semaphore()
    for z in sps:
        pl.semaphore_signal(barrier, inc=1, device_id={"space": z}, device_id_type=MESH)
    for q in dps:
        pl.semaphore_signal(barrier, inc=1, device_id={"dp": q}, device_id_type=MESH)
    pl.semaphore_wait(barrier, nsp + ndp - 2)

    def in_copy(a, j, z, slot, hf):
        return pltpu.make_async_remote_copy(
            src_ref=send.at[a, j, z, pl.ds(hf * part, part)],
            dst_ref=recv.at[a, j, slot, pl.ds(hf * part, part)],
            send_sem=in_send.at[a, j, z, hf],
            recv_sem=in_recv.at[a, j, slot, hf],
            device_id={"space": z},
            device_id_type=MESH,
        )

    def d_copy(j, z, slot, hf):
        return pltpu.make_async_remote_copy(
            src_ref=dsend.at[j, z, pl.ds(hf * part, part)],
            dst_ref=drecv.at[j, slot, pl.ds(hf * part, part)],
            send_sem=d_send.at[j, z, hf],
            recv_sem=d_recv.at[j, slot, hf],
            device_id={"space": z},
            device_id_type=MESH,
        )

    low = lax.broadcasted_iota(jnp.int32, (chunks * 16, 128), 1) < 64

    def pack(y, a, r):
        y = y.reshape(chunks, 2, 16, y.shape[-1])
        for q in range(nsp // 2):
            b = 384 * q

            def tile(t, half):
                return y[:, half, :, b + 128 * t : b + 128 * t + 128].reshape(chunks * 16, 128)

            def put(d, t, v):
                v = v.astype(BF).reshape(chunks, 16, 128)
                send[a, :, 2 * q + d, r, :, 128 * t : 128 * t + 128] = v

            b0, b1 = tile(1, 0), tile(1, 1)
            put(0, 0, tile(0, 0))
            put(0, 1, tile(0, 1))
            put(0, 2, jnp.where(low, b0, pltpu.roll(b1, 64, 1)))
            put(1, 0, tile(2, 0))
            put(1, 1, tile(2, 1))
            put(1, 2, jnp.where(low, pltpu.roll(b0, 64, 1), b1))

    def start_in(a, j, hf):
        for z in sps:
            in_copy(a, j, z, me, hf).start()
        at = pl.ds(hf * part, part)
        recv[a, j, me, at] = send[a, j, me, at]

    def grad_row(r, c):
        pack(jnp.dot(inv_ref[...], dout_ref[r], preferred_element_type=F32), 1, r)
        return c

    for hf in range(2):
        loads[hf].wait()
        lax.fori_loop(hf * part, (hf + 1) * part, grad_row, 0)
        start_in(1, 0, hf)

    gain = gain_ref[...].reshape(1, -1)
    channels = x_ref.shape[-1]

    def norm_row(r, c):
        v = x_ref[r].astype(F32)
        mean = jnp.mean(v, axis=-1, keepdims=True)
        v = v - mean
        rstd = lax.rsqrt(jnp.mean(v * v, axis=-1, keepdims=True) + norm_eps)
        mean_s[r] = mean
        rstd_s[r] = rstd
        v = v * rstd
        normed = (v * gain).astype(BF)
        pack(jnp.dot(fwd_ref[...], normed, preferred_element_type=F32), 0, r)
        prod = v * dout_ref[r].astype(F32)
        return c + jnp.sum(prod.reshape(-1, 8, channels), axis=0)

    gain_sum = jnp.zeros((8, channels), F32)
    for hf in range(2):
        loads[2 + hf].wait()
        gain_sum = lax.fori_loop(hf * part, (hf + 1) * part, norm_row, gain_sum)
        start_in(0, 0, hf)
    gain_a[me] = gain_sum
    for copy in loads[4:]:
        copy.wait()

    pick = e_ref[parity]
    fold = e2_ref[parity]
    mask = mask_ref[parity]
    for w_ref, out in ((win_ref, wci), (wout_ref, wco)):
        block = w_ref.shape[2]
        for p in range(2):
            w = jnp.dot(pick, w_ref[p], preferred_element_type=F32).astype(BF)
            w = lax.dot_general(w, fold[:, :block], NT, preferred_element_type=F32).astype(BF)
            w = w * mask
            if p == 0:
                out[:lanes, :lanes] = w
                out[lanes:, lanes:] = w
            else:
                out[:lanes, lanes:] = w
                out[lanes:, :lanes] = -w
    wide = lax.dot_general(
        bin_ref[...], pick.astype(F32), NT, precision=lax.Precision.HIGHEST,
        preferred_element_type=F32,
    )
    bias[:, :lanes] = wide[0:1]
    bias[:, lanes:] = wide[1:2]
    acc_in[...] = jnp.zeros_like(acc_in)
    acc_out[...] = jnp.zeros_like(acc_out)
    acc_b[...] = jnp.zeros_like(acc_b)
    acc_g[...] = jnp.zeros_like(acc_g)

    tile_rows = 128

    def middle(j):
        for a, out in ((1, gout), (0, modes)):
            for z in sps:
                for hf in range(2):
                    in_copy(a, j, z, z, hf).wait_recv()
            x = recv[a, j].reshape(2 * pos, lanes)
            for p in range(2):
                t = jnp.dot(m1_ref[p * pos : (p + 1) * pos], x, preferred_element_type=F32)
                out[:, p * lanes : (p + 1) * lanes] = t.astype(BF)

        def tile(t, c):
            at = pl.ds(pl.multiple_of(t * tile_rows, tile_rows), tile_rows)
            v = jnp.dot(modes[at], wci[...], preferred_element_type=F32) + bias[...]
            dh = lax.dot_general(gout[at], wco[...], NT, preferred_element_type=F32)
            tangent = jnp.tanh(root_coef * (v + cubic_coef * v * v * v))
            hidden[at] = (0.5 * v * (1.0 + tangent)).astype(BF)
            slope = 0.5 * (1.0 + tangent) + 0.5 * v * (1.0 - tangent * tangent) * root_coef * (
                1.0 + 3.0 * cubic_coef * v * v
            )
            d = (dh * slope).astype(BF)
            dpre[at] = d
            wide = d.astype(F32).reshape(tile_rows // 8, 8, 2 * lanes)
            acc_b[...] += jnp.sum(wide, axis=0)
            dm = lax.dot_general(d, wci[...], NT, preferred_element_type=F32).astype(BF)
            dmodes[at] = dm[:, :lanes]
            low_at = pl.ds(pl.multiple_of(pos + t * tile_rows, tile_rows), tile_rows)
            dmodes[low_at] = dm[:, lanes:]
            return c

        lax.fori_loop(0, pos // tile_rows, tile, 0)
        ds = jnp.dot(m2_ref[...], dmodes[...], preferred_element_type=F32).astype(BF)
        dsend[j] = ds.reshape(nsp, rows, 16, lanes)
        for hf in range(2):
            for z in sps:
                d_copy(j, z, me, hf).start()
        drecv[j, me] = dsend[j, me]
        cross = ds.astype(F32) * recv[0, j].reshape(2 * pos, lanes).astype(F32)
        acc_g[...] += jnp.sum(cross.reshape(-1, 8, lanes), axis=0)
        acc_out[...] += lax.dot_general(hidden[...], gout[...], TN, preferred_element_type=F32)
        acc_in[...] += lax.dot_general(modes[...], dpre[...], TN, preferred_element_type=F32)

    def step(j, c):
        @pl.when(j + 1 < chunks)
        def _():
            for a in (1, 0):
                for hf in range(2):
                    start_in(a, j + 1, hf)

        middle(j)
        return c

    lax.fori_loop(0, chunks, step, 0)

    local = e_ref.shape[2]
    shard = part_g.shape[1]
    pick32 = pick.astype(F32)
    fold32 = fold.astype(F32)
    mask32 = mask.astype(F32)
    sums_b = jnp.sum(acc_b[...], axis=0, keepdims=True)
    column = lax.broadcasted_iota(jnp.int32, (local, 128), 1)
    flat = []
    for n, acc in enumerate((acc_in, acc_out)):
        full = (
            acc[:lanes, :lanes] + acc[lanes:, lanes:],
            acc[:lanes, lanes:] - acc[lanes:, :lanes],
        )
        for p in range(2):
            g = lax.dot_general(
                pick32, full[p] * mask32, TN, precision=lax.Precision.HIGHEST,
                preferred_element_type=F32,
            )
            g = jnp.dot(g, fold32, precision=lax.Precision.HIGHEST, preferred_element_type=F32)
            if n == 0:
                db = lax.dot_general(
                    pick32, jnp.broadcast_to(sums_b[:, p * lanes : (p + 1) * lanes], (128, lanes)),
                    (((0,), (1,)), ((), ())), precision=lax.Precision.HIGHEST,
                    preferred_element_type=F32,
                )
                g = jnp.where(column == 96, db, g)
            per = local // shard
            part_g[(2 * n + p) * per : (2 * n + p + 1) * per] = g.reshape(per, shard, 128)

    def rs_copy(q, slot):
        return pltpu.make_async_remote_copy(
            src_ref=part_g.at[q],
            dst_ref=recv_g.at[slot],
            send_sem=rs_send.at[q],
            recv_sem=rs_recv.at[slot],
            device_id={"dp": q},
            device_id_type=MESH,
        )

    def ag_copy(q, slot):
        return pltpu.make_async_remote_copy(
            src_ref=gw_ref.at[dp],
            dst_ref=gw_ref.at[slot],
            send_sem=ag_send.at[q],
            recv_sem=ag_recv.at[slot],
            device_id={"dp": q},
            device_id_type=MESH,
        )

    for q in dps:
        rs_copy(q, dp).start()
    recv_g[dp] = part_g[dp]
    for q in dps:
        rs_copy(q, q).wait_recv()
    gw_ref[dp] = jnp.sum(recv_g[...], axis=0)
    for q in dps:
        ag_copy(q, dp).start()

    def ga_copy(z, slot):
        return pltpu.make_async_remote_copy(
            src_ref=gain_a.at[me],
            dst_ref=gain_a.at[slot],
            send_sem=ga_send.at[z],
            recv_sem=ga_recv.at[slot],
            device_id={"space": z},
            device_id_type=MESH,
        )

    def gb_copy(q, slot):
        return pltpu.make_async_remote_copy(
            src_ref=gain_b.at[dp],
            dst_ref=gain_b.at[slot],
            send_sem=gb_send.at[q],
            recv_sem=gb_recv.at[slot],
            device_id={"dp": q},
            device_id_type=MESH,
        )

    own = jnp.dot(acc_g[...], pick32, precision=lax.Precision.HIGHEST, preferred_element_type=F32)
    shift = lax.broadcasted_iota(jnp.int32, (local, channels), 1) == (
        lax.broadcasted_iota(jnp.int32, (local, channels), 0) + me * local
    )
    own = jnp.dot(
        own, shift.astype(F32), precision=lax.Precision.HIGHEST, preferred_element_type=F32
    )
    gain_a[me] = gain_a[me] + own / gain
    for z in sps:
        ga_copy(z, me).start()
    for z in sps:
        ga_copy(z, z).wait_recv()
    gain_b[dp] = jnp.sum(gain_a[...], axis=0)
    for q in dps:
        gb_copy(q, dp).start()
    for q in dps:
        gb_copy(q, q).wait_recv()
    gg_ref[...] = jnp.sum(jnp.sum(gain_b[...], axis=0), axis=0, keepdims=True)

    def last_row(r, c):
        for q in range(nsp // 2):
            b = 384 * q

            def tile(d, t):
                v = drecv[:, 2 * q + d, r, :, 128 * t : 128 * t + 128]
                return v.reshape(chunks * 16, 128)

            def put(half, t, v):
                v = v.astype(BF).reshape(chunks, 16, 128)
                dd[:, half, :, b + 128 * t : b + 128 * t + 128] = v

            e2, o2 = tile(0, 2).astype(F32), tile(1, 2).astype(F32)
            for half in range(2):
                put(half, 0, tile(0, half))
                put(half, 2, tile(1, half))
            put(0, 1, jnp.where(low, e2, pltpu.roll(o2, 64, 1)))
            put(1, 1, jnp.where(low, pltpu.roll(e2, 64, 1), o2))
        spectrum = dd[...].reshape(chunks * 32, dd.shape[-1])
        grad = jnp.dot(fin_ref[...], spectrum, preferred_element_type=F32)
        grad = grad + dout_ref[r].astype(F32)
        rstd = rstd_s[r]
        xhat = (x_ref[r].astype(F32) - mean_s[r]) * rstd
        scaled = grad * gain
        m_a = jnp.mean(scaled, axis=-1, keepdims=True)
        m_b = jnp.mean(scaled * xhat, axis=-1, keepdims=True)
        dx_ref[r] = (rstd * (scaled - m_a - xhat * m_b)).astype(BF)
        return c

    stores = []
    for hf in range(2):
        for j in range(chunks):
            for z in sps:
                d_copy(j, z, z, hf).wait_recv()
        lax.fori_loop(hf * part, (hf + 1) * part, last_row, 0)
        stores.append(
            pltpu.make_async_copy(halves(dx_ref, hf), halves(dx_hbm, hf), store_sem.at[hf])
        )
        stores[hf].start()

    for q in dps:
        ag_copy(q, q).wait_recv()
    for q in dps:
        rs_copy(q, dp).wait_send()
        ag_copy(q, dp).wait_send()
        gb_copy(q, dp).wait_send()
    for z in sps:
        ga_copy(z, me).wait_send()

    def drain(j, c):
        for z in sps:
            for hf in range(2):
                in_copy(0, j, z, me, hf).wait_send()
                in_copy(1, j, z, me, hf).wait_send()
                d_copy(j, z, me, hf).wait_send()
        return c

    lax.fori_loop(0, chunks, drain, 0)
    for copy in stores:
        copy.wait()


def finish(dx_in, gw_ref, gg_ref, dx_out, dwi_ref, db_ref, dwo_ref, dg_ref):
    dx_out[0] = dx_in[...]

    @pl.when(pl.program_id(0) == 0)
    def _():
        local, block = dwi_ref.shape[1:]
        eye = lax.broadcasted_iota(jnp.int32, (local, local), 0) == lax.broadcasted_iota(
            jnp.int32, (local, local), 1
        )
        for p in range(2):
            g = gw_ref[p]
            dwi_ref[p] = g[:, :block]
            dwo_ref[p] = gw_ref[2 + p][:, :block]
            db = jnp.where(eye, g[:, block : block + 1], 0.0)
            db_ref[p : p + 1] = jnp.sum(db, axis=0, keepdims=True)
        dg_ref[...] = gg_ref[...].reshape(dg_ref.shape)


def fused(ndp, nsp, inputs, gain, w_in, b_in, w_out, d_out):
    _, rows, width, channels = inputs.shape
    kept = width // 2
    height = rows * nsp
    local, block = w_in.shape[1], w_in.shape[2]
    chunks = kept // (2 * K8)
    lanes = 2 * local
    pos = height * K8
    shard = 4 * local // ndp
    fwd, inv, fin = column_tables(width, kept)
    m1, m2 = row_matrix(height)
    pick, fold, mask = lane_maps(local, block)
    vmem = pl.BlockSpec(memory_space=pltpu.VMEM)
    hbm = pl.BlockSpec(memory_space=pl.ANY)
    dma = pltpu.SemaphoreType.DMA
    dx, gw, gg = pl.pallas_call(
        functools.partial(kernel, ndp, nsp),
        out_shape=(
            jax.ShapeDtypeStruct((rows, width, channels), BF),
            jax.ShapeDtypeStruct((ndp, shard, 128), F32),
            jax.ShapeDtypeStruct((1, channels), F32),
        ),
        in_specs=[hbm] * 2 + [vmem] * 7 + [hbm] * 5,
        out_specs=(hbm, vmem, vmem),
        scratch_shapes=[
            pltpu.VMEM((2, chunks, nsp, rows, 16, lanes), BF),
            pltpu.VMEM((2, chunks, nsp, rows, 16, lanes), BF),
            pltpu.VMEM((chunks, nsp, rows, 16, lanes), BF),
            pltpu.VMEM((chunks, nsp, rows, 16, lanes), BF),
            pltpu.VMEM((2 * lanes, 2 * lanes), BF),
            pltpu.VMEM((2 * lanes, 2 * lanes), BF),
            pltpu.VMEM((1, 2 * lanes), F32),
            pltpu.VMEM((pos, 2 * lanes), BF),
            pltpu.VMEM((pos, 2 * lanes), BF),
            pltpu.VMEM((pos, 2 * lanes), BF),
            pltpu.VMEM((pos, 2 * lanes), BF),
            pltpu.VMEM((2 * pos, lanes), BF),
            pltpu.VMEM((2 * lanes, 2 * lanes), F32),
            pltpu.VMEM((2 * lanes, 2 * lanes), F32),
            pltpu.VMEM((8, 2 * lanes), F32),
            pltpu.VMEM((rows, width, 1), F32),
            pltpu.VMEM((rows, width, 1), F32),
            pltpu.VMEM((chunks, 2, 16, channels), BF),
            pltpu.VMEM((ndp, shard, 128), F32),
            pltpu.VMEM((ndp, shard, 128), F32),
            pltpu.VMEM((nsp, 8, channels), F32),
            pltpu.VMEM((ndp, 8, channels), F32),
            pltpu.VMEM((8, lanes), F32),
            pltpu.VMEM((rows, width, channels), BF),
            pltpu.VMEM((rows, width, channels), BF),
            pltpu.VMEM(m1.shape, BF),
            pltpu.VMEM(m2.shape, BF),
            pltpu.VMEM(pick.shape, BF),
            pltpu.VMEM(fold.shape, BF),
            pltpu.VMEM(mask.shape, BF),
            pltpu.VMEM((rows, width, channels), BF),
            dma((9,)),
            dma((2,)),
            dma((2, chunks, nsp, 2)),
            dma((2, chunks, nsp, 2)),
            dma((chunks, nsp, 2)),
            dma((chunks, nsp, 2)),
            dma((ndp,)),
            dma((ndp,)),
            dma((ndp,)),
            dma((ndp,)),
            dma((nsp,)),
            dma((nsp,)),
            dma((ndp,)),
            dma((ndp,)),
        ],
        compiler_params=pltpu.CompilerParams(
            collective_id=0, has_side_effects=True, vmem_limit_bytes=60 * 1024 * 1024
        ),
    )(
        inputs[0],
        d_out[0],
        gain,
        w_in,
        b_in,
        w_out,
        *(jnp.asarray(v) for v in (fwd, inv, fin, m1, m2, pick, fold, mask)),
    )
    gw = gw.reshape(4, local, 128)
    step = 2

    def whole(shape):
        return pl.BlockSpec(shape, lambda i: (0,) * len(shape))

    return pl.pallas_call(
        finish,
        grid=(rows // step,),
        out_shape=(
            jax.ShapeDtypeStruct((1, rows, width, channels), BF),
            jax.ShapeDtypeStruct((2, local, block), F32),
            jax.ShapeDtypeStruct((2, local), F32),
            jax.ShapeDtypeStruct((2, local, block), F32),
            jax.ShapeDtypeStruct((channels,), F32),
        ),
        in_specs=[
            pl.BlockSpec((step, width, channels), lambda i: (i, 0, 0)),
            whole((4, local, 128)),
            whole((1, channels)),
        ],
        out_specs=(
            pl.BlockSpec((1, step, width, channels), lambda i: (0, i, 0, 0)),
            whole((2, local, block)),
            whole((2, local)),
            whole((2, local, block)),
            whole((channels,)),
        ),
    )(dx, gw, gg)


def choose(ndp, nsp, *args):
    inputs, w_in = args[0], args[2]
    local, block = w_in.shape[1], w_in.shape[2]
    fits = (
        inputs.shape[0] == 1
        and nsp == 4
        and local == 192
        and block == 96
        and inputs.shape[1] % 2 == 0
        and inputs.shape[2] % 32 == 0
        and inputs.shape[1] * nsp * K8 % 128 == 0
        and local % (4 * local // ndp) == 0
        and (4 * local // ndp) % 8 == 0
    )
    if fits:
        return fused(ndp, nsp, *args)
    return on_device(*args)


def solution(mesh):
    return jax.shard_map(
        functools.partial(choose, mesh.shape["dp"], mesh.shape["space"]),
        mesh=mesh,
        in_specs=(
            P("dp", "space", None, None),
            P(),
            P(None, "space", None),
            P(None, "space"),
            P(None, "space", None),
            P("dp", "space", None, None),
        ),
        out_specs=(
            P("dp", "space", None, None),
            P(None, "space", None),
            P(None, "space"),
            P(None, "space", None),
            P(),
        ),
        check_vma=False,
    )
```

```python
import functools
import math

import jax
import jax.numpy as jnp
import ml_dtypes
import numpy as np
from jax import lax
from jax.experimental import pallas as pl
from jax.experimental.pallas import tpu as pltpu
from jax.sharding import PartitionSpec as P

norm_eps = 1e-05
root_coef = math.sqrt(2.0 / math.pi)
cubic_coef = 0.044715


def dft_tables(length, kept):
    index_rows = jnp.arange(length, dtype=jnp.int32)
    index_cols = jnp.arange(kept, dtype=jnp.int32)
    product = index_rows[:, None] * index_cols[None, :] % length
    angles = 2.0 * math.pi / length * product.astype(jnp.float32)
    scale = 1.0 / math.sqrt(length)
    return (jnp.cos(angles) * scale, jnp.sin(angles) * scale)


def half_signs(kept):
    return jnp.concatenate([jnp.ones((kept,), jnp.float32), -jnp.ones((kept,), jnp.float32)])


def swap_parts(values, signs):
    return jnp.roll(values, values.shape[-1] // 2, axis=-1) * signs.astype(values.dtype)


def rows_apply(spectra, row_tables, signs):
    paired = jnp.einsum("tgh,shcm->tsgcm", row_tables, spectra, preferred_element_type=jnp.float32)
    return paired[0] + swap_parts(paired[1], signs)


def block_apply(values, weights, signs):
    real_part = jnp.einsum(
        "sgbim,bio->sgbom", values, weights[0], preferred_element_type=jnp.float32
    )
    imag_part = jnp.einsum(
        "sgbim,bio->sgbom", values, weights[1], preferred_element_type=jnp.float32
    )
    return real_part + swap_parts(imag_part, signs)


def block_adjoint(values, weights, signs):
    real_part = jnp.einsum(
        "sgbom,bio->sgbim", values, weights[0], preferred_element_type=jnp.float32
    )
    imag_part = jnp.einsum(
        "sgbom,bio->sgbim", values, weights[1], preferred_element_type=jnp.float32
    )
    return real_part + swap_parts(imag_part, signs)


def block_weight_grad(inputs_spec, grads_spec, signs):
    real_part = jnp.einsum(
        "sgbim,sgbom->bio", inputs_spec, grads_spec, preferred_element_type=jnp.float32
    )
    imag_part = jnp.einsum(
        "sgbim,sgbom->bio",
        swap_parts(inputs_spec, signs),
        grads_spec,
        preferred_element_type=jnp.float32,
    )
    return jnp.stack([real_part, imag_part])


def gelu_value(values):
    inner = root_coef * (values + cubic_coef * values * values * values)
    return 0.5 * values * (1.0 + jnp.tanh(inner))


def gelu_slope(values):
    inner = root_coef * (values + cubic_coef * values * values * values)
    tangent = jnp.tanh(inner)
    return 0.5 * (1.0 + tangent) + 0.5 * values * (1.0 - tangent * tangent) * root_coef * (
        1.0 + 3.0 * cubic_coef * values * values
    )


def on_device(inputs, gain, w_in, b_in, w_out, d_out):
    samples, rows, width, channels = inputs.shape
    kept = width // 2
    height = rows * lax.axis_size("space")
    local_channels = w_in.shape[1]
    block = w_in.shape[2]
    groups = local_channels // block
    cos_rows, sin_rows = dft_tables(height, height)
    row_tables = jnp.stack([cos_rows, sin_rows]).astype(jnp.bfloat16)
    cos_cols, sin_cols = dft_tables(width, kept)
    forward_cols = jnp.concatenate([cos_cols, -sin_cols], axis=1).astype(jnp.bfloat16)
    doubling = jnp.where(jnp.arange(kept, dtype=jnp.int32) == 0, 1.0, 2.0).astype(jnp.float32)
    inverse_cols = jnp.concatenate([cos_cols * doubling, -sin_cols * doubling], axis=1).astype(
        jnp.bfloat16
    )
    plus_minus = half_signs(kept)
    minus_plus = -plus_minus
    weights_in = w_in.reshape(2, groups, block, block)
    weights_out = w_out.reshape(2, groups, block, block)
    bias_parts = b_in.reshape(2, groups, block)
    bias_full = jnp.concatenate(
        [
            jnp.broadcast_to(bias_parts[0][:, :, None], (groups, block, kept)),
            jnp.broadcast_to(bias_parts[1][:, :, None], (groups, block, kept)),
        ],
        axis=-1,
    )
    values = inputs.astype(jnp.float32)
    centre = jnp.mean(values, axis=-1, keepdims=True)
    mean_removed = values - centre
    variance = jnp.mean(mean_removed * mean_removed, axis=-1, keepdims=True)
    reciprocal_scale = lax.rsqrt(variance + norm_eps)
    standardized_input = mean_removed * reciprocal_scale
    normalized_input = (standardized_input * gain).astype(jnp.bfloat16)
    spectrum_cols = jnp.einsum(
        "srwc,wm->srcm", normalized_input, forward_cols, preferred_element_type=jnp.float32
    ).astype(jnp.bfloat16)
    spectrum_full = lax.all_to_all(spectrum_cols, "space", split_axis=2, concat_axis=1, tiled=True)
    modes = rows_apply(spectrum_full, row_tables, plus_minus).astype(jnp.bfloat16)
    modes = modes.reshape(samples, height, groups, block, width)
    preact = block_apply(modes, weights_in, minus_plus) + bias_full
    hidden = gelu_value(preact).astype(jnp.bfloat16)
    grad_cols = jnp.einsum(
        "srwc,wm->srcm", d_out, inverse_cols, preferred_element_type=jnp.float32
    ).astype(jnp.bfloat16)
    grad_full = lax.all_to_all(grad_cols, "space", split_axis=2, concat_axis=1, tiled=True)
    grad_out = rows_apply(grad_full, row_tables, plus_minus).astype(jnp.bfloat16)
    grad_out = grad_out.reshape(samples, height, groups, block, width)
    grad_w_out = block_weight_grad(hidden, grad_out, minus_plus)
    d_hidden = block_adjoint(grad_out, weights_out, plus_minus)
    d_preact = (d_hidden * gelu_slope(preact)).astype(jnp.bfloat16)
    grad_w_in = block_weight_grad(modes, d_preact, minus_plus)
    bias_sums = jnp.sum(
        d_preact.reshape(samples, height, groups, block, 2, kept), axis=(0, 1, 5), dtype=jnp.float32
    )
    grad_b_in = jnp.moveaxis(bias_sums, 2, 0).reshape(2, local_channels)
    d_modes = block_adjoint(d_preact, weights_in, plus_minus).astype(jnp.bfloat16)
    d_modes = d_modes.reshape(samples, height, local_channels, width)
    d_spectrum = rows_apply(d_modes, row_tables, minus_plus).astype(jnp.bfloat16)
    d_cols = lax.all_to_all(d_spectrum, "space", split_axis=1, concat_axis=2, tiled=True)
    d_filter = jnp.einsum("srcm,wm->srwc", d_cols, forward_cols, preferred_element_type=jnp.float32)
    normalized_gradient = d_out.astype(jnp.float32) + d_filter
    gain_component = jnp.sum(normalized_gradient * standardized_input, axis=(0, 1, 2))
    rescaled_output = normalized_gradient * gain
    value_gradient = reciprocal_scale * (
        rescaled_output
        - jnp.mean(rescaled_output, axis=-1, keepdims=True)
        - standardized_input
        * jnp.mean(rescaled_output * standardized_input, axis=-1, keepdims=True)
    )
    d_inputs = value_gradient.astype(jnp.bfloat16)
    flat_w_in = grad_w_in.reshape(2, local_channels, block)
    flat_w_out = grad_w_out.reshape(2, local_channels, block)
    sum_w_in, sum_b_in, sum_w_out = lax.psum((flat_w_in, grad_b_in, flat_w_out), "dp")
    sum_gain = lax.psum(gain_component, ("dp", "space"))
    return (d_inputs, sum_w_in, sum_b_in, sum_w_out, sum_gain)


MESH = pl.DeviceIdType.MESH
BF = jnp.bfloat16
F32 = jnp.float32
NT = (((1,), (1,)), ((), ()))
TN = (((0,), (0,)), ((), ()))
K8 = 8


def np_tables(length, kept):
    product = (np.arange(length)[:, None] * np.arange(kept)[None, :]) % length
    angles = (2.0 * np.pi / length) * product
    scale = 1.0 / np.sqrt(length)
    return np.cos(angles) * scale, np.sin(angles) * scale


def narrow(table):
    return table.astype(np.float32).astype(ml_dtypes.bfloat16)


def column_tables(width, kept):
    cos, sin = np_tables(width, kept)
    order = np.arange(width)
    wave = (order // (4 * K8)) * (2 * K8) + (order // (2 * K8)) % 2 * K8 + order % K8
    part = (order // K8) % 2
    forward = np.where(part[:, None] == 0, cos.T[wave], -sin.T[wave])
    double = np.where(wave == 0, 1.0, 2.0)[:, None]
    return narrow(forward), narrow(forward * double), narrow(forward.T)


def row_matrix(height):
    cos, sin = np_tables(height, height)
    row = np.arange(2 * height * K8)
    rp, rg, rk = row // (height * K8), row % (height * K8) // K8, row % K8
    cp, ch, ck = row // K8 % 2, row // (2 * K8), row % K8
    c = cos[rg[:, None], ch[None, :]]
    s = sin[rg[:, None], ch[None, :]]
    signed = np.where(rp[:, None] < cp[None, :], s, -s)
    full = np.where(rp[:, None] == cp[None, :], c, signed)
    full = np.where(rk[:, None] == ck[None, :], full, 0.0)
    return narrow(full), narrow(full.T)


def lane_maps(local, block):
    picks, folds, masks = [], [], []
    lane = np.arange(2 * local)
    wide = lane < 256
    half = np.where(wide, lane // 128, (lane - 256) // 64)
    even = np.where(wide, lane % 128, 128 + lane % 64)
    odd = np.where(wide, 64 + lane % 128, lane % 64)
    for channel in (even, odd):
        picks.append(channel[:, None] == np.arange(local)[None, :])
        folds.append(channel[:, None] % block == np.arange(128)[None, :])
        group = channel // block
        masks.append(
            (half[:, None] == half[None, :]) & (group[:, None] == group[None, :])
        )
    return tuple(narrow(np.stack(v)) for v in (picks, folds, masks))


def kernel(
    ndp,
    nsp,
    x_hbm,
    dout_hbm,
    gain_ref,
    win_ref,
    bin_ref,
    wout_ref,
    fwd_ref,
    inv_ref,
    fin_ref,
    m1_hbm,
    m2_hbm,
    e_hbm,
    e2_hbm,
    mask_hbm,
    dx_hbm,
    gw_ref,
    gg_ref,
    send,
    recv,
    dsend,
    drecv,
    wci,
    wco,
    bias,
    modes,
    gout,
    hidden,
    dpre,
    dmodes,
    acc_in,
    acc_out,
    acc_b,
    mean_s,
    rstd_s,
    dd,
    part_g,
    recv_g,
    gain_a,
    gain_b,
    acc_g,
    x_ref,
    dout_ref,
    m1_ref,
    m2_ref,
    e_ref,
    e2_ref,
    mask_ref,
    dx_ref,
    load_sem,
    store_sem,
    in_send,
    in_recv,
    d_send,
    d_recv,
    rs_send,
    rs_recv,
    ag_send,
    ag_recv,
    ga_send,
    ga_recv,
    gb_send,
    gb_recv,
):
    dp = lax.axis_index("dp")
    me = lax.axis_index("space")
    rows = x_ref.shape[0]
    chunks = send.shape[1]
    pos = modes.shape[0]
    lanes = wci.shape[0] // 2
    sps = [lax.rem(me + o, nsp) for o in range(1, nsp)]
    dps = [lax.rem(dp + o, ndp) for o in range(1, ndp)]
    parity = lax.rem(me, 2)
    part = rows // 3

    def load(n, src, dst):
        return pltpu.make_async_copy(src, dst, load_sem.at[n])

    def halves(ref, hf):
        return ref.at[pl.ds(hf * part, part)]

    loads = [load(hf, halves(dout_hbm, hf), halves(dout_ref, hf)) for hf in range(3)]
    loads += [load(3 + hf, halves(x_hbm, hf), halves(x_ref, hf)) for hf in range(3)]
    pairs = ((e_hbm, e_ref), (e2_hbm, e2_ref), (mask_hbm, mask_ref), (m1_hbm, m1_ref), (m2_hbm, m2_ref))
    loads += [load(6 + n, src, dst) for n, (src, dst) in enumerate(pairs)]
    for copy in loads:
        copy.start()

    barrier = pltpu.get_barrier_semaphore()
    for z in sps:
        pl.semaphore_signal(barrier, inc=1, device_id={"space": z}, device_id_type=MESH)
    for q in dps:
        pl.semaphore_signal(barrier, inc=1, device_id={"dp": q}, device_id_type=MESH)
    pl.semaphore_wait(barrier, nsp + ndp - 2)

    def in_copy(a, j, z, slot, hf):
        return pltpu.make_async_remote_copy(
            src_ref=send.at[a, j, z, pl.ds(hf * part, part)],
            dst_ref=recv.at[a, j, slot, pl.ds(hf * part, part)],
            send_sem=in_send.at[a, j, z, hf],
            recv_sem=in_recv.at[a, j, slot, hf],
            device_id={"space": z},
            device_id_type=MESH,
        )

    def d_copy(j, z, slot, hf):
        return pltpu.make_async_remote_copy(
            src_ref=dsend.at[j, z, pl.ds(hf * part, part)],
            dst_ref=drecv.at[j, slot, pl.ds(hf * part, part)],
            send_sem=d_send.at[j, z, hf],
            recv_sem=d_recv.at[j, slot, hf],
            device_id={"space": z},
            device_id_type=MESH,
        )

    low = lax.broadcasted_iota(jnp.int32, (chunks * 16, 128), 1) < 64

    def pack(y, a, r):
        y = y.reshape(chunks, 2, 16, y.shape[-1])
        for q in range(nsp // 2):
            b = 384 * q

            def tile(t, half):
                return y[:, half, :, b + 128 * t : b + 128 * t + 128].reshape(chunks * 16, 128)

            def put(d, t, v):
                v = v.astype(BF).reshape(chunks, 16, 128)
                send[a, :, 2 * q + d, r, :, 128 * t : 128 * t + 128] = v

            b0, b1 = tile(1, 0), tile(1, 1)
            put(0, 0, tile(0, 0))
            put(0, 1, tile(0, 1))
            put(0, 2, jnp.where(low, b0, pltpu.roll(b1, 64, 1)))
            put(1, 0, tile(2, 0))
            put(1, 1, tile(2, 1))
            put(1, 2, jnp.where(low, pltpu.roll(b0, 64, 1), b1))

    def start_in(a, j, hf):
        for z in sps:
            in_copy(a, j, z, me, hf).start()
        at = pl.ds(hf * part, part)
        recv[a, j, me, at] = send[a, j, me, at]

    def grad_row(r, c):
        pack(jnp.dot(inv_ref[...], dout_ref[r], preferred_element_type=F32), 1, r)
        return c

    for hf in range(3):
        loads[hf].wait()
        lax.fori_loop(hf * part, (hf + 1) * part, grad_row, 0)
        start_in(1, 0, hf)

    gain = gain_ref[...].reshape(1, -1)
    channels = x_ref.shape[-1]

    def norm_row(r, c):
        v = x_ref[r].astype(F32)
        mean = jnp.mean(v, axis=-1, keepdims=True)
        v = v - mean
        rstd = lax.rsqrt(jnp.mean(v * v, axis=-1, keepdims=True) + norm_eps)
        mean_s[r] = mean
        rstd_s[r] = rstd
        v = v * rstd
        normed = (v * gain).astype(BF)
        pack(jnp.dot(fwd_ref[...], normed, preferred_element_type=F32), 0, r)
        prod = v * dout_ref[r].astype(F32)
        return c + jnp.sum(prod.reshape(-1, 8, channels), axis=0)

    gain_sum = jnp.zeros((8, channels), F32)
    for hf in range(3):
        loads[3 + hf].wait()
        gain_sum = lax.fori_loop(hf * part, (hf + 1) * part, norm_row, gain_sum)
        start_in(0, 0, hf)
    gain_a[me] = gain_sum
    for copy in loads[6:]:
        copy.wait()

    pick = e_ref[parity]
    fold = e2_ref[parity]
    mask = mask_ref[parity]
    for w_ref, out in ((win_ref, wci), (wout_ref, wco)):
        block = w_ref.shape[2]
        for p in range(2):
            w = jnp.dot(pick, w_ref[p], preferred_element_type=F32).astype(BF)
            w = lax.dot_general(w, fold[:, :block], NT, preferred_element_type=F32).astype(BF)
            w = w * mask
            if p == 0:
                out[:lanes, :lanes] = w
                out[lanes:, lanes:] = w
            else:
                out[:lanes, lanes:] = w
                out[lanes:, :lanes] = -w
    wide = lax.dot_general(
        bin_ref[...], pick.astype(F32), NT, precision=lax.Precision.HIGHEST,
        preferred_element_type=F32,
    )
    bias[:, :lanes] = wide[0:1]
    bias[:, lanes:] = wide[1:2]
    acc_in[...] = jnp.zeros_like(acc_in)
    acc_out[...] = jnp.zeros_like(acc_out)
    acc_b[...] = jnp.zeros_like(acc_b)
    acc_g[...] = jnp.zeros_like(acc_g)

    tile_rows = 128

    def middle(j):
        for a, out in ((1, gout), (0, modes)):
            for z in sps:
                for hf in range(3):
                    in_copy(a, j, z, z, hf).wait_recv()
            x = recv[a, j].reshape(2 * pos, lanes)
            for p in range(2):
                t = jnp.dot(m1_ref[p * pos : (p + 1) * pos], x, preferred_element_type=F32)
                out[:, p * lanes : (p + 1) * lanes] = t.astype(BF)

        def tile(t, c):
            at = pl.ds(pl.multiple_of(t * tile_rows, tile_rows), tile_rows)
            v = jnp.dot(modes[at], wci[...], preferred_element_type=F32) + bias[...]
            dh = lax.dot_general(gout[at], wco[...], NT, preferred_element_type=F32)
            tangent = jnp.tanh(root_coef * (v + cubic_coef * v * v * v))
            hidden[at] = (0.5 * v * (1.0 + tangent)).astype(BF)
            slope = 0.5 * (1.0 + tangent) + 0.5 * v * (1.0 - tangent * tangent) * root_coef * (
                1.0 + 3.0 * cubic_coef * v * v
            )
            d = (dh * slope).astype(BF)
            dpre[at] = d
            wide = d.astype(F32).reshape(tile_rows // 8, 8, 2 * lanes)
            acc_b[...] += jnp.sum(wide, axis=0)
            dm = lax.dot_general(d, wci[...], NT, preferred_element_type=F32).astype(BF)
            dmodes[at] = dm[:, :lanes]
            low_at = pl.ds(pl.multiple_of(pos + t * tile_rows, tile_rows), tile_rows)
            dmodes[low_at] = dm[:, lanes:]
            return c

        lax.fori_loop(0, pos // tile_rows, tile, 0)
        ds = jnp.dot(m2_ref[...], dmodes[...], preferred_element_type=F32).astype(BF)
        dsend[j] = ds.reshape(nsp, rows, 16, lanes)
        for hf in range(3):
            for z in sps:
                d_copy(j, z, me, hf).start()
        drecv[j, me] = dsend[j, me]
        cross = ds.astype(F32) * recv[0, j].reshape(2 * pos, lanes).astype(F32)
        acc_g[...] += jnp.sum(cross.reshape(-1, 8, lanes), axis=0)
        acc_out[...] += lax.dot_general(hidden[...], gout[...], TN, preferred_element_type=F32)
        acc_in[...] += lax.dot_general(modes[...], dpre[...], TN, preferred_element_type=F32)

    def step(j, c):
        @pl.when(j + 1 < chunks)
        def _():
            for a in (1, 0):
                for hf in range(3):
                    start_in(a, j + 1, hf)

        middle(j)
        return c

    lax.fori_loop(0, chunks, step, 0)

    local = e_ref.shape[2]
    shard = part_g.shape[1]
    pick32 = pick.astype(F32)
    fold32 = fold.astype(F32)
    mask32 = mask.astype(F32)
    sums_b = jnp.sum(acc_b[...], axis=0, keepdims=True)
    column = lax.broadcasted_iota(jnp.int32, (local, 128), 1)
    flat = []
    for n, acc in enumerate((acc_in, acc_out)):
        full = (
            acc[:lanes, :lanes] + acc[lanes:, lanes:],
            acc[:lanes, lanes:] - acc[lanes:, :lanes],
        )
        for p in range(2):
            g = lax.dot_general(
                pick32, full[p] * mask32, TN, precision=lax.Precision.HIGHEST,
                preferred_element_type=F32,
            )
            g = jnp.dot(g, fold32, precision=lax.Precision.HIGHEST, preferred_element_type=F32)
            if n == 0:
                db = lax.dot_general(
                    pick32, jnp.broadcast_to(sums_b[:, p * lanes : (p + 1) * lanes], (128, lanes)),
                    (((0,), (1,)), ((), ())), precision=lax.Precision.HIGHEST,
                    preferred_element_type=F32,
                )
                g = jnp.where(column == 96, db, g)
            per = local // shard
            part_g[(2 * n + p) * per : (2 * n + p + 1) * per] = g.reshape(per, shard, 128)

    def rs_copy(q, slot):
        return pltpu.make_async_remote_copy(
            src_ref=part_g.at[q],
            dst_ref=recv_g.at[slot],
            send_sem=rs_send.at[q],
            recv_sem=rs_recv.at[slot],
            device_id={"dp": q},
            device_id_type=MESH,
        )

    def ag_copy(q, slot):
        return pltpu.make_async_remote_copy(
            src_ref=gw_ref.at[dp],
            dst_ref=gw_ref.at[slot],
            send_sem=ag_send.at[q],
            recv_sem=ag_recv.at[slot],
            device_id={"dp": q},
            device_id_type=MESH,
        )

    for q in dps:
        rs_copy(q, dp).start()
    recv_g[dp] = part_g[dp]
    for q in dps:
        rs_copy(q, q).wait_recv()
    gw_ref[dp] = jnp.sum(recv_g[...], axis=0)
    for q in dps:
        ag_copy(q, dp).start()

    def ga_copy(z, slot):
        return pltpu.make_async_remote_copy(
            src_ref=gain_a.at[me],
            dst_ref=gain_a.at[slot],
            send_sem=ga_send.at[z],
            recv_sem=ga_recv.at[slot],
            device_id={"space": z},
            device_id_type=MESH,
        )

    def gb_copy(q, slot):
        return pltpu.make_async_remote_copy(
            src_ref=gain_b.at[dp],
            dst_ref=gain_b.at[slot],
            send_sem=gb_send.at[q],
            recv_sem=gb_recv.at[slot],
            device_id={"dp": q},
            device_id_type=MESH,
        )

    own = jnp.dot(acc_g[...], pick32, precision=lax.Precision.HIGHEST, preferred_element_type=F32)
    shift = lax.broadcasted_iota(jnp.int32, (local, channels), 1) == (
        lax.broadcasted_iota(jnp.int32, (local, channels), 0) + me * local
    )
    own = jnp.dot(
        own, shift.astype(F32), precision=lax.Precision.HIGHEST, preferred_element_type=F32
    )
    gain_a[me] = gain_a[me] + own / gain
    for z in sps:
        ga_copy(z, me).start()
    for z in sps:
        ga_copy(z, z).wait_recv()
    gain_b[dp] = jnp.sum(gain_a[...], axis=0)
    for q in dps:
        gb_copy(q, dp).start()
    for q in dps:
        gb_copy(q, q).wait_recv()
    gg_ref[...] = jnp.sum(jnp.sum(gain_b[...], axis=0), axis=0, keepdims=True)

    def last_row(r, c):
        for q in range(nsp // 2):
            b = 384 * q

            def tile(d, t):
                v = drecv[:, 2 * q + d, r, :, 128 * t : 128 * t + 128]
                return v.reshape(chunks * 16, 128)

            def put(half, t, v):
                v = v.astype(BF).reshape(chunks, 16, 128)
                dd[:, half, :, b + 128 * t : b + 128 * t + 128] = v

            e2, o2 = tile(0, 2).astype(F32), tile(1, 2).astype(F32)
            for half in range(2):
                put(half, 0, tile(0, half))
                put(half, 2, tile(1, half))
            put(0, 1, jnp.where(low, e2, pltpu.roll(o2, 64, 1)))
            put(1, 1, jnp.where(low, pltpu.roll(e2, 64, 1), o2))
        spectrum = dd[...].reshape(chunks * 32, dd.shape[-1])
        grad = jnp.dot(fin_ref[...], spectrum, preferred_element_type=F32)
        grad = grad + dout_ref[r].astype(F32)
        rstd = rstd_s[r]
        xhat = (x_ref[r].astype(F32) - mean_s[r]) * rstd
        scaled = grad * gain
        m_a = jnp.mean(scaled, axis=-1, keepdims=True)
        m_b = jnp.mean(scaled * xhat, axis=-1, keepdims=True)
        dx_ref[r] = (rstd * (scaled - m_a - xhat * m_b)).astype(BF)
        return c

    stores = []
    for hf in range(3):
        for j in range(chunks):
            for z in sps:
                d_copy(j, z, z, hf).wait_recv()
        lax.fori_loop(hf * part, (hf + 1) * part, last_row, 0)
        stores.append(
            pltpu.make_async_copy(halves(dx_ref, hf), halves(dx_hbm, hf), store_sem.at[hf])
        )
        stores[hf].start()

    for q in dps:
        ag_copy(q, q).wait_recv()
    for q in dps:
        rs_copy(q, dp).wait_send()
        ag_copy(q, dp).wait_send()
        gb_copy(q, dp).wait_send()
    for z in sps:
        ga_copy(z, me).wait_send()

    def drain(j, c):
        for z in sps:
            for hf in range(3):
                in_copy(0, j, z, me, hf).wait_send()
                in_copy(1, j, z, me, hf).wait_send()
                d_copy(j, z, me, hf).wait_send()
        return c

    lax.fori_loop(0, chunks, drain, 0)
    for copy in stores:
        copy.wait()


def finish(dx_in, gw_ref, gg_ref, dx_out, dwi_ref, db_ref, dwo_ref, dg_ref):
    dx_out[0] = dx_in[...]

    @pl.when(pl.program_id(0) == 0)
    def _():
        local, block = dwi_ref.shape[1:]
        eye = lax.broadcasted_iota(jnp.int32, (local, local), 0) == lax.broadcasted_iota(
            jnp.int32, (local, local), 1
        )
        for p in range(2):
            g = gw_ref[p]
            dwi_ref[p] = g[:, :block]
            dwo_ref[p] = gw_ref[2 + p][:, :block]
            db = jnp.where(eye, g[:, block : block + 1], 0.0)
            db_ref[p : p + 1] = jnp.sum(db, axis=0, keepdims=True)
        dg_ref[...] = gg_ref[...].reshape(dg_ref.shape)


def fused(ndp, nsp, inputs, gain, w_in, b_in, w_out, d_out):
    _, rows, width, channels = inputs.shape
    kept = width // 2
    height = rows * nsp
    local, block = w_in.shape[1], w_in.shape[2]
    chunks = kept // (2 * K8)
    lanes = 2 * local
    pos = height * K8
    shard = 4 * local // ndp
    fwd, inv, fin = column_tables(width, kept)
    m1, m2 = row_matrix(height)
    pick, fold, mask = lane_maps(local, block)
    vmem = pl.BlockSpec(memory_space=pltpu.VMEM)
    hbm = pl.BlockSpec(memory_space=pl.ANY)
    dma = pltpu.SemaphoreType.DMA
    dx, gw, gg = pl.pallas_call(
        functools.partial(kernel, ndp, nsp),
        out_shape=(
            jax.ShapeDtypeStruct((rows, width, channels), BF),
            jax.ShapeDtypeStruct((ndp, shard, 128), F32),
            jax.ShapeDtypeStruct((1, channels), F32),
        ),
        in_specs=[hbm] * 2 + [vmem] * 7 + [hbm] * 5,
        out_specs=(hbm, vmem, vmem),
        scratch_shapes=[
            pltpu.VMEM((2, chunks, nsp, rows, 16, lanes), BF),
            pltpu.VMEM((2, chunks, nsp, rows, 16, lanes), BF),
            pltpu.VMEM((chunks, nsp, rows, 16, lanes), BF),
            pltpu.VMEM((chunks, nsp, rows, 16, lanes), BF),
            pltpu.VMEM((2 * lanes, 2 * lanes), BF),
            pltpu.VMEM((2 * lanes, 2 * lanes), BF),
            pltpu.VMEM((1, 2 * lanes), F32),
            pltpu.VMEM((pos, 2 * lanes), BF),
            pltpu.VMEM((pos, 2 * lanes), BF),
            pltpu.VMEM((pos, 2 * lanes), BF),
            pltpu.VMEM((pos, 2 * lanes), BF),
            pltpu.VMEM((2 * pos, lanes), BF),
            pltpu.VMEM((2 * lanes, 2 * lanes), F32),
            pltpu.VMEM((2 * lanes, 2 * lanes), F32),
            pltpu.VMEM((8, 2 * lanes), F32),
            pltpu.VMEM((rows, width, 1), F32),
            pltpu.VMEM((rows, width, 1), F32),
            pltpu.VMEM((chunks, 2, 16, channels), BF),
            pltpu.VMEM((ndp, shard, 128), F32),
            pltpu.VMEM((ndp, shard, 128), F32),
            pltpu.VMEM((nsp, 8, channels), F32),
            pltpu.VMEM((ndp, 8, channels), F32),
            pltpu.VMEM((8, lanes), F32),
            pltpu.VMEM((rows, width, channels), BF),
            pltpu.VMEM((rows, width, channels), BF),
            pltpu.VMEM(m1.shape, BF),
            pltpu.VMEM(m2.shape, BF),
            pltpu.VMEM(pick.shape, BF),
            pltpu.VMEM(fold.shape, BF),
            pltpu.VMEM(mask.shape, BF),
            pltpu.VMEM((rows, width, channels), BF),
            dma((11,)),
            dma((3,)),
            dma((2, chunks, nsp, 3)),
            dma((2, chunks, nsp, 3)),
            dma((chunks, nsp, 3)),
            dma((chunks, nsp, 3)),
            dma((ndp,)),
            dma((ndp,)),
            dma((ndp,)),
            dma((ndp,)),
            dma((nsp,)),
            dma((nsp,)),
            dma((ndp,)),
            dma((ndp,)),
        ],
        compiler_params=pltpu.CompilerParams(
            collective_id=0, has_side_effects=True, vmem_limit_bytes=60 * 1024 * 1024
        ),
    )(
        inputs[0],
        d_out[0],
        gain,
        w_in,
        b_in,
        w_out,
        *(jnp.asarray(v) for v in (fwd, inv, fin, m1, m2, pick, fold, mask)),
    )
    gw = gw.reshape(4, local, 128)
    step = 4

    def whole(shape):
        return pl.BlockSpec(shape, lambda i: (0,) * len(shape))

    return pl.pallas_call(
        finish,
        grid=(rows // step,),
        out_shape=(
            jax.ShapeDtypeStruct((1, rows, width, channels), BF),
            jax.ShapeDtypeStruct((2, local, block), F32),
            jax.ShapeDtypeStruct((2, local), F32),
            jax.ShapeDtypeStruct((2, local, block), F32),
            jax.ShapeDtypeStruct((channels,), F32),
        ),
        in_specs=[
            pl.BlockSpec((step, width, channels), lambda i: (i, 0, 0)),
            whole((4, local, 128)),
            whole((1, channels)),
        ],
        out_specs=(
            pl.BlockSpec((1, step, width, channels), lambda i: (0, i, 0, 0)),
            whole((2, local, block)),
            whole((2, local)),
            whole((2, local, block)),
            whole((channels,)),
        ),
    )(dx, gw, gg)


def choose(ndp, nsp, *args):
    inputs, w_in = args[0], args[2]
    local, block = w_in.shape[1], w_in.shape[2]
    fits = (
        inputs.shape[0] == 1
        and nsp == 4
        and local == 192
        and block == 96
        and inputs.shape[1] % 12 == 0
        and inputs.shape[2] % 32 == 0
        and inputs.shape[1] * nsp * K8 % 128 == 0
        and local % (4 * local // ndp) == 0
        and (4 * local // ndp) % 8 == 0
    )
    if fits:
        return fused(ndp, nsp, *args)
    return on_device(*args)


def solution(mesh):
    return jax.shard_map(
        functools.partial(choose, mesh.shape["dp"], mesh.shape["space"]),
        mesh=mesh,
        in_specs=(
            P("dp", "space", None, None),
            P(),
            P(None, "space", None),
            P(None, "space"),
            P(None, "space", None),
            P("dp", "space", None, None),
        ),
        out_specs=(
            P("dp", "space", None, None),
            P(None, "space", None),
            P(None, "space"),
            P(None, "space", None),
            P(),
        ),
        check_vma=False,
    )
```
